32 devices in a mesh: cuts: 4 (over x, core), tile: 8 (over z, y).
Axes of the slice: x: 2, y: 2, z: 4, core: 2. Of those that a mesh axis runs over, the one named last changes fastest.
Arguments:
- state_in: float32 [4, 2, 128, 1024], P('cuts', None, 'tile'), may hold values from -0.625 to 0.625
- sea_depth: float32 [128, 1024], P('tile'), may hold values from 1.5 to 3
- pressure: float32 [128, 1024], P('tile'), may hold values from -3 to 3
Outputs:
- state_out: float32 [4, 2, 128, 1024], P('cuts', None, 'tile')
The draws below stay inside these ranges and needn't reach their ends.
All inputs are finite; a program needn't handle non-finite values.
Results may differ from the reference program's by a relative error of at most 0.0003.
Values sent between devices are 32-bit elements; how exact they have to be, the bound alone decides.
A program may use at most 64 MiB of HBM per device.

```python
import jax
import jax.numpy as jnp

NY = 1024
LEVELS = 8
DEFECT = 3
SLICES = 4
NX = 128


def draw_sea_depth(key, part):
    across = jnp.arange(NX, dtype=jnp.float32)[:, None] / max(NX - 1, 1)
    incline = 1.8 + 0.8 * across
    roughness = jax.random.uniform(key, (NX, NY), jnp.float32, 0.8, 1.25)
    return jnp.clip(incline * roughness, 1.5, 3.0).astype(jnp.float32)


def level_of(key, extent, shards, least, high):
    def one(dim, shards_of):
        draws = jax.random.uniform(jax.random.fold_in(jax.random.fold_in(key, 6), dim), (shards_of,), jnp.float32, least / len(shards), high / len(shards))
        return jnp.repeat(jnp.exp(draws), extent[dim] // shards_of).reshape((-1,) + (1,) * (len(extent) - dim - 1))

    gain = one(*shards[0])
    for cut in shards[1:]:
        gain = gain * one(*cut)
    return gain


def gaussian(key, shape, spread, reach, pieces=(), kind=jnp.bfloat16):
    gain = level_of(key, shape, pieces, -0.22, 0.18) if pieces else 1.0
    drawn = jax.random.normal(key, shape, jnp.float32) * spread * gain
    return jnp.minimum(jnp.maximum(drawn, -reach), reach).astype(kind)


def setup_inputs(seed: int = 0) -> dict:
    keys = jax.random.split(jax.random.key(seed), 4)
    return {
        "state_in": gaussian(keys[0], (SLICES, 2, NX, NY), 0.25, 0.625, ((0, 4), (2, 8)), jnp.float32),
        "sea_depth": draw_sea_depth(jax.random.fold_in(keys[3], 71), 0),
        "pressure": gaussian(keys[2], (NX, NY), 0.5, 3.0, ((0, 8),), jnp.float32),
    }


TIME_STEP = 0.8
SHIP_SPEED = 0.5
EPSILON = 1e-06

def horizontal(padded):
    middle = padded[..., 1:-1, :]
    widened = jnp.pad(middle, [(0, 0)] * (middle.ndim - 1) + [(1, 1)])
    return padded[..., 2:, :] + padded[..., :-2, :] + widened[..., 2:] + widened[..., :-2] - 4.0 * middle

def vertical_part(potential, surface, vertical):
    above = jnp.concatenate([potential[1:], surface[None]], axis=0)
    below = jnp.concatenate([potential[1:2], potential[:-1]], axis=0)
    return vertical * (above - 2.0 * potential + below)

def operator(padded, surface, vertical):
    return horizontal(padded) + vertical_part(padded[:, 1:-1, :], surface, vertical)

def elimination(vertical):
    diagonal = -2.0 * vertical - 4.0
    inverses = [1.0 / diagonal]
    ratios = [2.0 * vertical * inverses[0]]
    for level in range(1, LEVELS):
        inverse = 1.0 / (diagonal - vertical * ratios[-1])
        inverses.append(inverse)
        ratios.append(vertical * inverse)
    return (inverses, ratios)

def tridiagonal(residual, vertical, factors):
    inverses, ratios = factors
    forward = [residual[0] * inverses[0]]
    for level in range(1, LEVELS):
        forward.append((residual[level] - vertical * forward[-1]) * inverses[level])
    solution = [forward[-1]]
    for level in range(LEVELS - 2, -1, -1):
        solution.append(forward[level] - ratios[level] * solution[-1])
    return jnp.stack(solution[::-1])

def pad_rows(values):
    return jnp.pad(values, ((0, 0), (1, 1), (0, 0)))

def tendency(state, sea_depth, pressure, vertical, factors):
    elevation, potential_top = (state[0], state[1])
    potential = jnp.broadcast_to(potential_top, (LEVELS,) + potential_top.shape)
    residual = -operator(pad_rows(potential), potential_top, vertical)
    flat_zero = jnp.zeros_like(potential_top)
    for sweep in range(DEFECT):
        correction = tridiagonal(residual, vertical, factors)
        image = operator(pad_rows(correction), flat_zero, vertical)
        step_size = jnp.sum(residual * image) / (jnp.sum(image * image) + EPSILON)
        potential = potential + step_size * correction
        if sweep + 1 < DEFECT:
            residual = residual - step_size * image
    vertical_vel = (3.0 * potential_top - 4.0 * potential[-1] + potential[-2]) * LEVELS / (2.0 * sea_depth)
    padded = pad_rows(state)
    east = (padded[:, 2:, :] - padded[:, :-2, :]) * 0.5
    widened = jnp.pad(state, ((0, 0), (0, 0), (1, 1)))
    north = (widened[:, :, 2:] - widened[:, :, :-2]) * 0.5
    slope_sq = east[0] * east[0] + north[0] * north[0]
    height_rate = SHIP_SPEED * east[0] - (east[0] * east[1] + north[0] * north[1]) + vertical_vel * (1.0 + slope_sq)
    flow_rate = SHIP_SPEED * east[1] - elevation - 0.5 * (east[1] * east[1] + north[1] * north[1]) + 0.5 * vertical_vel * vertical_vel * (1.0 + slope_sq) - pressure
    return jnp.stack([height_rate, flow_rate])

def runge_kutta(state, sea_depth, pressure, vertical, factors):
    rate_one = tendency(state, sea_depth, pressure, vertical, factors)
    rate_two = tendency(state + 0.5 * TIME_STEP * rate_one, sea_depth, pressure, vertical, factors)
    rate_three = tendency(state + 0.5 * TIME_STEP * rate_two, sea_depth, pressure, vertical, factors)
    rate_four = tendency(state + TIME_STEP * rate_three, sea_depth, pressure, vertical, factors)
    return state + TIME_STEP / 6.0 * (rate_one + 2.0 * rate_two + 2.0 * rate_three + rate_four)

def coarse_matrix(sea_depth):
    stiffness = jnp.tanh(sea_depth)
    frequency = jnp.sqrt(stiffness)
    cosine = jnp.cos(TIME_STEP * frequency)
    sine_part = jnp.sin(TIME_STEP * frequency)
    return (cosine, stiffness * sine_part / frequency, -sine_part / frequency, cosine)

def coarse_apply(coarse, state):
    return jnp.stack([coarse[0] * state[0] + coarse[1] * state[1], coarse[2] * state[0] + coarse[3] * state[1]])

def reference(state_in, sea_depth, pressure):
    vertical = (LEVELS / sea_depth) ** 2
    factors = elimination(vertical)
    coarse = coarse_matrix(sea_depth)
    defects = []
    for slice_index in range(SLICES):
        fine_state = runge_kutta(state_in[slice_index], sea_depth, pressure, vertical, factors)
        defects.append(fine_state - coarse_apply(coarse, state_in[slice_index]))
    current = state_in[0]
    results = []
    for slice_index in range(SLICES):
        current = coarse_apply(coarse, current) + defects[slice_index]
        results.append(current)
    return jnp.stack(results)
```

```python
import functools
import math

import jax
import jax.numpy as jnp
from jax import lax
from jax.experimental import pallas as pl
from jax.experimental.pallas import tpu as pltpu
from jax.sharding import PartitionSpec as P

LEVELS = 8
STAGES = 4
TIME_STEP = 0.8
SHIP_SPEED = 0.5
EPSILON = 1e-06
MESH = pl.DeviceIdType.MESH
SUB = 8
LANE = 128
NSUM = 10
FOLD = 5
WIDE = 13
EXTRA = [10, 7, 4, 0]

THETA = [(m + 0.5) * math.pi / LEVELS for m in range(LEVELS)]
LAM = [2.0 * math.cos(t) - 2.0 for t in THETA]
WEIGHT = [(-1.0) ** m / math.tan(t / 2) / LEVELS for m, t in enumerate(THETA)]
TOPROW = [
    (math.cos((LEVELS - 2) * t) - 4.0 * math.cos((LEVELS - 1) * t)) * w
    for t, w in zip(THETA, WEIGHT)
]


def masks(shape):
    lane = lax.broadcasted_iota(jnp.int32, shape, len(shape) - 1)
    sub = lax.broadcasted_iota(jnp.int32, shape, len(shape) - 2)
    first = lane == 0
    last = lane == LANE - 1
    return first, first & (sub == 0), last, last & (sub == SUB - 1)


def before(v, mask):
    first, start, _, _ = mask
    r = pltpu.roll(v, 1, axis=2)
    return jnp.where(start, 0.0, jnp.where(first, pltpu.roll(r, 1, axis=1), r))


def after(v, mask):
    _, _, last, end = mask
    r = pltpu.roll(v, LANE - 1, axis=2)
    return jnp.where(end, 0.0, jnp.where(last, pltpu.roll(r, SUB - 1, axis=1), r))


def neighbours(v):
    mid = v[1:-1]
    mask = masks(mid.shape)
    return (v[2:] + v[:-2]) + (before(mid, mask) + after(mid, mask))


def step_sizes(g):
    g00, g01, g02, g03, g11, g12, g13, g22, g23, g33 = g
    gram = [[g00, g01, g02, g03], [g01, g11, g12, g13], [g02, g12, g22, g23], [g03, g13, g23, g33]]

    def quad(c, left, right):
        total = None
        for i, ci in enumerate(c):
            for j, cj in enumerate(c):
                if left == right and j < i:
                    continue
                term = ci * cj * gram[i + left][j + right]
                if left == right and j > i:
                    term = 2.0 * term
                total = term if total is None else total + term
        return total

    coef = [jnp.ones_like(g00)]
    beta = [0.0, 0.0, 0.0]
    for sweep in range(3):
        rr = quad(coef, 0, 0)
        re = quad(coef, 0, 1)
        ee = quad(coef, 1, 1)
        inv = 1.0 / (jnp.maximum(rr + 2.0 * re + ee, 0.0) + EPSILON)
        s = (rr + re) * inv
        t = (re + ee + EPSILON) * inv
        for j, c in enumerate(coef):
            beta[j] = beta[j] + s * c
        nxt = [t * c for c in coef] + [jnp.zeros_like(s)]
        for j, c in enumerate(coef):
            nxt[j + 1] = nxt[j + 1] - s * c
        coef = nxt
    return beta


def kernel(
    tiles, slices, rows, state_ref, depth_ref, press_ref, out_ref,
    raw, raw_d, raw_p, x, dm, wfac, coarse, first, total, planes, edge, part, slots, chain, chain_in,
    load_s, halo_s, halo_r, sum_s, sum_r, chain_s, chain_r,
):
    me = lax.axis_index("tile")
    cut = lax.axis_index("cuts")
    has_lo = me > 0
    has_hi = me < tiles - 1
    has_prev = cut > 0
    has_next = cut < slices - 1
    chunks = [(a, min(4, rows - a)) for a in range(0, rows, 4)]
    end = WIDE + rows

    loads = [
        pltpu.make_async_copy(state_ref.at[0], raw, load_s.at[0]),
        pltpu.make_async_copy(depth_ref, raw_d, load_s.at[1]),
        pltpu.make_async_copy(press_ref, raw_p, load_s.at[2]),
    ]
    for load in loads:
        load.start()

    x[:, 0:WIDE] = jnp.zeros((4, WIDE, SUB, LANE), jnp.float32)
    x[:, end : end + WIDE] = jnp.zeros((4, WIDE, SUB, LANE), jnp.float32)

    barrier = pltpu.get_barrier_semaphore()
    for d in range(1, tiles):
        pl.semaphore_signal(
            barrier, inc=1, device_id={"tile": lax.rem(me + d, tiles)}, device_id_type=MESH
        )

    @pl.when(has_prev)
    def _():
        pl.semaphore_signal(barrier, inc=1, device_id={"cuts": cut - 1}, device_id_type=MESH)

    @pl.when(has_next)
    def _():
        pl.semaphore_signal(barrier, inc=1, device_id={"cuts": cut + 1}, device_id_type=MESH)

    for load in loads:
        load.wait()
    for j in range(SUB):
        cols = slice(j * LANE, (j + 1) * LANE)
        x[0, WIDE:end, j, :] = raw[1, :, cols]
        x[1, WIDE:end, j, :] = raw_d[:, cols]
        x[2, WIDE:end, j, :] = raw[0, :, cols]
        x[3, WIDE:end, j, :] = raw_p[:, cols]

    parts = [(0, 2, 0, 4), (0, 2, 4, WIDE - 4), (2, 2, 0, WIDE - 2)]

    def halo_copy(k, side):
        p, np_, a, size = parts[k]
        if side == 0:
            src, dst = WIDE + a, end + a
        else:
            src, dst = end - a - size, WIDE - a - size
        return pltpu.make_async_remote_copy(
            src_ref=x.at[pl.ds(p, np_), pl.ds(src, size)],
            dst_ref=x.at[pl.ds(p, np_), pl.ds(dst, size)],
            send_sem=halo_s.at[k, side],
            recv_sem=halo_r.at[k, side],
            device_id={"tile": me - 1 if side == 0 else me + 1},
            device_id_type=MESH,
        )

    def halo_both(k, act):
        @pl.when(has_lo)
        def _():
            act(k, 0)

        @pl.when(has_hi)
        def _():
            act(k, 1)

    start = lambda k, side: halo_copy(k, side).start()
    arrive = lambda k, side: halo_copy(k, 1 - side).wait_recv()
    leave = lambda k, side: halo_copy(k, side).wait_send()

    def columns(a, b, inside):
        safe = x[1, a:b]
        if inside is not None:
            safe = jnp.where(inside, safe, 1.0)
        vert = LEVELS / safe
        vert = vert * vert
        for m in range(LEVELS):
            inverse = 1.0 / (vert * LAM[m] - 4.0)
            dm[m, a:b] = inverse if inside is None else jnp.where(inside, inverse, 0.0)
        wfac[a:b] = (0.5 * LEVELS) / safe

    columns(WIDE, end, None)
    own = x[1, WIDE:end]
    stiff = jnp.tanh(own)
    z = TIME_STEP * TIME_STEP * stiff
    cosine = 1.0 + z * (-1 / 2 + z * (1 / 24 + z * (-1 / 720 + z * (1 / 40320 - z / 3628800))))
    sine = TIME_STEP * (
        1.0 + z * (-1 / 6 + z * (1 / 120 + z * (-1 / 5040 + z * (1 / 362880 - z / 39916800))))
    )
    coarse[0] = cosine
    coarse[1] = stiff * sine
    coarse[2] = -sine

    pl.semaphore_wait(
        barrier, tiles - 1 + has_prev.astype(jnp.int32) + has_next.astype(jnp.int32)
    )
    for k in range(3):
        halo_both(k, start)

    halo_both(0, arrive)
    columns(WIDE - 3, WIDE, has_lo)
    columns(end, end + 3, has_hi)

    def sum_copy(s, d):
        return pltpu.make_async_remote_copy(
            src_ref=part.at[s],
            dst_ref=slots.at[s, d],
            send_sem=sum_s.at[s, d],
            recv_sem=sum_r.at[s, d],
            device_id={"tile": lax.rem(me + d, tiles)},
            device_id_type=MESH,
        )

    half = lax.broadcasted_iota(jnp.int32, (1, LANE), 1) < LANE // 2

    def inner_products(s):
        top = x[0, WIDE - 4 : end + 4]
        r0 = 4.0 * top[1:-1] - neighbours(top)
        u0 = r0[3:-3]
        gram = [None] * 9
        for m in range(LEVELS):
            c0 = dm[m, WIDE - 3 : end + 3] * r0
            u1 = neighbours(c0)
            c1 = dm[m, WIDE - 2 : end + 2] * u1
            u2 = neighbours(c1)
            c2 = dm[m, WIDE - 1 : end + 1] * u2
            u3 = neighbours(c2)
            us = [u0, u1[2:-2], u2[1:-1], u3]
            cs = [c0[3:-3], c1[2:-2], c2[1:-1]]
            k = 0
            for i in range(4):
                for j in range(max(i, 1), 4):
                    p = (4.0 * WEIGHT[m] ** 2) * jnp.sum(us[i] * us[j], axis=0)
                    gram[k] = p if gram[k] is None else gram[k] + p
                    k += 1
            for i in range(3):
                a = WEIGHT[m] * us[i + 1]
                b = TOPROW[m] * cs[i]
                if m == 0:
                    planes[i] = a
                    planes[3 + i] = b
                else:
                    planes[i] += a
                    planes[3 + i] += b
        bottom = [u0, planes[0], planes[1], planes[2]]
        k = 0
        for i in range(4):
            for j in range(max(i, 1), 4):
                gram[k] = gram[k] + 0.5 * jnp.sum(bottom[i] * bottom[j], axis=0)
                k += 1
        gram = [LEVELS * jnp.sum(u0 * u0, axis=0)] + gram
        gram = [jnp.sum(g, axis=0, keepdims=True) for g in gram]
        for k in range(FOLD):
            a, b = gram[k], gram[k + FOLD]
            part[s, k : k + 1] = jnp.where(half, a, b) + pltpu.roll(
                jnp.where(half, b, a), LANE // 2, axis=1
            )

    def beyond(side, a, b):
        top = x[0, a - 3 : b + 3]
        r0 = 4.0 * top[1:-1] - neighbours(top)
        size = b - a
        for m in range(LEVELS):
            c0 = dm[m, a - 2 : b + 2] * r0
            c1 = dm[m, a - 1 : b + 1] * neighbours(c0)
            c2 = dm[m, a:b] * neighbours(c1)
            for i, c in enumerate([c0[2:-2], c1[1:-1], c2]):
                v = TOPROW[m] * c
                if m == 0:
                    edge[side, i, 0:size] = v
                else:
                    edge[side, i, 0:size] += v

    def explicit(a, b):
        elev = x[2, a:b]
        phi = x[0, a:b]
        mask = masks(elev.shape)
        he = 0.5 * (x[2, a + 1 : b + 1] - x[2, a - 1 : b - 1])
        fe = 0.5 * (x[0, a + 1 : b + 1] - x[0, a - 1 : b - 1])
        hn = 0.5 * (after(elev, mask) - before(elev, mask))
        fn = 0.5 * (after(phi, mask) - before(phi, mask))
        slope = 1.0 + he * he + hn * hn
        rate_h = SHIP_SPEED * he - (he * fe + hn * fn)
        rate_f = SHIP_SPEED * fe - elev - 0.5 * (fe * fe + fn * fn) - x[3, a:b]
        return slope, rate_h, rate_f

    for s in range(STAGES):
        extra = EXTRA[s]
        inner_products(s)
        for d in range(1, tiles):
            sum_copy(s, d).start()

        if s == 0:
            halo_both(1, arrive)
            halo_both(2, arrive)
            columns(1, WIDE - 3, has_lo)
            columns(end + 3, end + WIDE - 1, has_hi)
            first[0] = x[2]
            first[1] = x[0]
        regions = [(WIDE, end, None)]
        if extra:
            beyond(0, WIDE - extra, WIDE)
            beyond(1, end, end + extra)
            regions += [(WIDE - extra, WIDE, 0), (end, end + extra, 1)]
        known = [explicit(a, b) for a, b, _ in regions]
        if s == 0:
            for k in range(3):
                halo_both(k, leave)

        for d in range(1, tiles):
            sum_copy(s, d).wait_recv()
        whole = part[s]
        for d in range(1, tiles):
            whole = whole + slots[s, d]
        low = jnp.sum(jnp.where(half, whole, 0.0), axis=1, keepdims=True)
        high = jnp.sum(jnp.where(half, 0.0, whole), axis=1, keepdims=True)
        sums = [low[k : k + 1] for k in range(FOLD)] + [high[k : k + 1] for k in range(FOLD)]
        beta = [jnp.broadcast_to(b, (SUB, LANE)) for b in step_sizes(sums)]

        share = (1.0 if s in (0, STAGES - 1) else 2.0) * (TIME_STEP / 6.0)
        ahead = TIME_STEP if s == STAGES - 2 else 0.5 * TIME_STEP
        for (a, b, side), (slope, rate_h, rate_f) in zip(regions, known):
            if side is None:
                y = [planes[3 + i] for i in range(3)]
            else:
                y = [edge[side, i, 0 : b - a] for i in range(3)]
            w = (beta[0] * y[0] + beta[1] * y[1] + beta[2] * y[2]) * wfac[a:b]
            ws = w * slope
            rate_h = rate_h + ws
            rate_f = rate_f + 0.5 * w * ws
            if side is None:
                if s == 0:
                    total[0] = first[0, a:b] + share * rate_h
                    total[1] = first[1, a:b] + share * rate_f
                else:
                    total[0] += share * rate_h
                    total[1] += share * rate_f
            if s < STAGES - 1:
                new_h = first[0, a:b] + ahead * rate_h
                new_f = first[1, a:b] + ahead * rate_f
                if side is not None:
                    there = has_hi if side else has_lo
                    new_h = jnp.where(there, new_h, 0.0)
                    new_f = jnp.where(there, new_f, 0.0)
                x[2, a:b] = new_h
                x[0, a:b] = new_f

    def chain_copy(k):
        a, size = chunks[k]
        return pltpu.make_async_remote_copy(
            src_ref=chain.at[pl.ds(a, size)],
            dst_ref=chain_in.at[pl.ds(a, size)],
            send_sem=chain_s.at[k],
            recv_sem=chain_r.at[k],
            device_id={"cuts": cut + 1},
            device_id_type=MESH,
        )

    @pl.when(has_prev)
    def _():
        e = first[0, WIDE:end]
        p = first[1, WIDE:end]
        total[0] = total[0] - (coarse[0] * e + coarse[1] * p)
        total[1] = total[1] - (coarse[2] * e + coarse[0] * p)

    for k, (a, size) in enumerate(chunks):
        span = slice(a, a + size)

        @pl.when(has_prev)
        def _():
            chain_copy(k).wait_recv()
            e = chain_in[span, 0]
            p = chain_in[span, 1]
            chain[span, 0] = coarse[0, span] * e + coarse[1, span] * p + total[0, span]
            chain[span, 1] = coarse[2, span] * e + coarse[0, span] * p + total[1, span]

        @pl.when(jnp.logical_not(has_prev))
        def _():
            chain[span, 0] = total[0, span]
            chain[span, 1] = total[1, span]

        @pl.when(has_next)
        def _():
            chain_copy(k).start()

    for j in range(SUB):
        cols = slice(j * LANE, (j + 1) * LANE)
        for c in range(2):
            out_ref[0, c, :, cols] = chain[:, c, j, :]

    @pl.when(has_next)
    def _():
        for k in range(len(chunks)):
            chain_copy(k).wait_send()

    for s in range(STAGES):
        for d in range(1, tiles):
            sum_copy(s, d).wait_send()


def local(tiles, slices, state_in, sea_depth, pressure):
    rows = sea_depth.shape[0]
    plane = (rows, SUB, LANE)
    wide = rows + 2 * WIDE
    f32 = jnp.float32
    chunks = -(-rows // 4)
    return pl.pallas_call(
        functools.partial(kernel, tiles, slices, rows),
        out_shape=jax.ShapeDtypeStruct(state_in.shape, f32),
        in_specs=[pl.BlockSpec(memory_space=pltpu.HBM)] * 3,
        out_specs=pl.BlockSpec(memory_space=pltpu.VMEM),
        scratch_shapes=[
            pltpu.VMEM(state_in.shape[1:], f32),
            pltpu.VMEM(sea_depth.shape, f32),
            pltpu.VMEM(pressure.shape, f32),
            pltpu.VMEM((4, wide, SUB, LANE), f32),
            pltpu.VMEM((LEVELS, wide, SUB, LANE), f32),
            pltpu.VMEM((wide, SUB, LANE), f32),
            pltpu.VMEM((3,) + plane, f32),
            pltpu.VMEM((2, wide, SUB, LANE), f32),
            pltpu.VMEM((2,) + plane, f32),
            pltpu.VMEM((6,) + plane, f32),
            pltpu.VMEM((2, 3, EXTRA[0], SUB, LANE), f32),
            pltpu.VMEM((STAGES, FOLD, LANE), f32),
            pltpu.VMEM((STAGES, tiles, FOLD, LANE), f32),
            pltpu.VMEM((rows, 2, SUB, LANE), f32),
            pltpu.VMEM((rows, 2, SUB, LANE), f32),
            pltpu.SemaphoreType.DMA((3,)),
            pltpu.SemaphoreType.DMA((3, 2)),
            pltpu.SemaphoreType.DMA((3, 2)),
            pltpu.SemaphoreType.DMA((STAGES, tiles)),
            pltpu.SemaphoreType.DMA((STAGES, tiles)),
            pltpu.SemaphoreType.DMA((chunks,)),
            pltpu.SemaphoreType.DMA((chunks,)),
        ],
        compiler_params=pltpu.CompilerParams(
            collective_id=0, has_side_effects=True, vmem_limit_bytes=60 * 1024 * 1024
        ),
        name="wake_step",
    )(state_in, sea_depth, pressure)


def solution(mesh):
    placed = (P("cuts", None, "tile", None), P("tile", None), P("tile", None))
    return jax.shard_map(
        functools.partial(local, mesh.shape["tile"], mesh.shape["cuts"]),
        mesh=mesh,
        in_specs=placed,
        out_specs=P("cuts", None, "tile", None),
        check_vma=False,
    )
```

```python
import functools
import math

import jax
import jax.numpy as jnp
from jax import lax
from jax.experimental import pallas as pl
from jax.experimental.pallas import tpu as pltpu
from jax.sharding import PartitionSpec as P

LEVELS = 8
STAGES = 4
TIME_STEP = 0.8
SHIP_SPEED = 0.5
EPSILON = 1e-06
MESH = pl.DeviceIdType.MESH
SUB = 8
LANE = 128
FOLD = 5
PAD = 16
SPAN = 24
PARTS = [(0, 2, 0, 4), (0, 2, 4, 3), (2, 2, 0, 5), (0, 2, 7, 6), (2, 2, 5, 6)]
NEAR_PARTS = [1, 2]
FAR_PARTS = [3, 4]

THETA = [(m + 0.5) * math.pi / LEVELS for m in range(LEVELS)]
LAM = [2.0 * math.cos(t) - 2.0 for t in THETA]
WEIGHT = [(-1.0) ** m / math.tan(t / 2) / LEVELS for m, t in enumerate(THETA)]
TOPROW = [math.cos((LEVELS - 2) * t) - 4.0 * math.cos((LEVELS - 1) * t) for t in THETA]


def rolled(v):
    lane = lax.broadcasted_iota(jnp.int32, (1,) + v.shape[1:], 2)
    r = pltpu.roll(v, 1, axis=2)
    l = pltpu.roll(v, LANE - 1, axis=2)
    zero = jnp.zeros_like(v[:1])
    before = jnp.where(lane == 0, jnp.concatenate([zero, r[:-1]], axis=0), r)
    after = jnp.where(lane == LANE - 1, jnp.concatenate([l[1:], zero], axis=0), l)
    return before, after


def rows8(ref, a):
    return ref[:, a : a + SUB]


def neighbours(ref, a):
    before, after = rolled(rows8(ref, a))
    return (rows8(ref, a + 1) + rows8(ref, a - 1)) + (before + after)


def step_sizes(g):
    g00, g01, g02, g03, g11, g12, g13, g22, g23, g33 = g
    gram = [[g00, g01, g02, g03], [g01, g11, g12, g13], [g02, g12, g22, g23], [g03, g13, g23, g33]]

    def quad(c, left, right):
        total = None
        for i, ci in enumerate(c):
            for j, cj in enumerate(c):
                if left == right and j < i:
                    continue
                term = ci * cj * gram[i + left][j + right]
                if left == right and j > i:
                    term = 2.0 * term
                total = term if total is None else total + term
        return total

    coef = [jnp.ones_like(g00)]
    beta = [0.0, 0.0, 0.0]
    for sweep in range(3):
        rr = quad(coef, 0, 0)
        re = quad(coef, 0, 1)
        ee = quad(coef, 1, 1)
        inv = 1.0 / (jnp.maximum(rr + 2.0 * re + ee, 0.0) + EPSILON)
        s = (rr + re) * inv
        t = (re + ee + EPSILON) * inv
        for j, c in enumerate(coef):
            beta[j] = beta[j] + s * c
        nxt = [t * c for c in coef] + [jnp.zeros_like(s)]
        for j, c in enumerate(coef):
            nxt[j + 1] = nxt[j + 1] - s * c
        coef = nxt
    return beta


def kernel(
    tiles, slices, rows, state_ref, depth_ref, press_ref, out_ref,
    raw, raw_d, raw_p, x, later, dm, dw, wfac, coarse, total, res, c, u, planes, top, out_c, out_y,
    part, slots, chain, chain_in,
    load_s, halo_s, halo_r, sum_s, sum_r, chain_s, chain_r,
):
    me = lax.axis_index("tile")
    cut = lax.axis_index("cuts")
    has_lo = me > 0
    has_hi = me < tiles - 1
    has_prev = cut > 0
    has_next = cut < slices - 1
    blocks = x.shape[1]
    end = PAD + rows
    own = list(range(PAD, end, SUB))
    wide = list(range(PAD - 3, end - 5, SUB)) + [end - 5]
    wide = sorted(set(wide))

    loads = [
        pltpu.make_async_copy(state_ref.at[0], raw, load_s.at[0]),
        pltpu.make_async_copy(depth_ref, raw_d, load_s.at[1]),
        pltpu.make_async_copy(press_ref, raw_p, load_s.at[2]),
    ]
    for load in loads:
        load.start()

    for p in range(4):
        x[p, :, 0:PAD] = jnp.zeros((blocks, PAD, LANE), jnp.float32)
        x[p, :, end : end + PAD] = jnp.zeros((blocks, PAD, LANE), jnp.float32)

    barrier = pltpu.get_barrier_semaphore()
    for d in range(1, tiles):
        pl.semaphore_signal(
            barrier, inc=1, device_id={"tile": lax.rem(me + d, tiles)}, device_id_type=MESH
        )

    @pl.when(has_prev)
    def _():
        pl.semaphore_signal(barrier, inc=1, device_id={"cuts": cut - 1}, device_id_type=MESH)

    @pl.when(has_next)
    def _():
        pl.semaphore_signal(barrier, inc=1, device_id={"cuts": cut + 1}, device_id_type=MESH)

    for load in loads:
        load.wait()
    for j in range(blocks):
        cols = slice(j * LANE, (j + 1) * LANE)
        x[0, j, PAD:end] = raw[1, :, cols]
        x[1, j, PAD:end] = raw_d[:, cols]
        x[2, j, PAD:end] = raw[0, :, cols]
        x[3, j, PAD:end] = raw_p[:, cols]

    def halo_copy(k, side):
        p, count, a, size = PARTS[k]
        if side == 0:
            src, dst = PAD + a, end + a
        else:
            src, dst = end - a - size, PAD - a - size
        return pltpu.make_async_remote_copy(
            src_ref=x.at[pl.ds(p, count), :, pl.ds(src, size)],
            dst_ref=x.at[pl.ds(p, count), :, pl.ds(dst, size)],
            send_sem=halo_s.at[k, side],
            recv_sem=halo_r.at[k, side],
            device_id={"tile": me - 1 if side == 0 else me + 1},
            device_id_type=MESH,
        )

    def halo_both(ks, act):
        @pl.when(has_lo)
        def _():
            for k in ks:
                act(k, 0)

        @pl.when(has_hi)
        def _():
            for k in ks:
                act(k, 1)

    start = lambda k, side: halo_copy(k, side).start()
    arrive = lambda k, side: halo_copy(k, 1 - side).wait_recv()
    leave = lambda k, side: halo_copy(k, side).wait_send()

    def columns(a, inside=None):
        safe = rows8(x.at[1], a)
        if inside is not None:
            safe = jnp.where(inside, safe, 1.0)
        inv_depth = 1.0 / safe
        vert = LEVELS * inv_depth
        vert = vert * vert
        for m in range(LEVELS):
            inverse = 1.0 / (vert * LAM[m] - 4.0)
            if inside is not None:
                inverse = jnp.where(inside, inverse, 0.0)
            dm[m, :, a : a + SUB] = inverse
            dw[m, :, a : a + SUB] = WEIGHT[m] * inverse
        wfac[:, a : a + SUB] = (0.5 * LEVELS) * inv_depth

    sub = lax.broadcasted_iota(jnp.int32, (1, SUB, LANE), 1)

    def edge_columns(a_lo, own_lo, a_hi, own_hi):
        columns(a_lo, sub + SUB * has_lo.astype(jnp.int32) >= own_lo)
        columns(a_hi, sub - SUB * has_hi.astype(jnp.int32) < own_hi)

    for a in own:
        columns(a)

    pl.semaphore_wait(
        barrier, tiles - 1 + has_prev.astype(jnp.int32) + has_next.astype(jnp.int32)
    )
    halo_both([0], start)
    halo_both(NEAR_PARTS, start)

    depth = x[1, :, PAD:end]
    stiff = jnp.tanh(depth)
    z = TIME_STEP * TIME_STEP * stiff
    coarse[0] = 1.0 + z * (-1 / 2 + z * (1 / 24 + z * (-1 / 720 + z * (1 / 40320 - z / 3628800))))
    sine = TIME_STEP * (
        1.0 + z * (-1 / 6 + z * (1 / 120 + z * (-1 / 5040 + z * (1 / 362880 - z / 39916800))))
    )
    coarse[1] = stiff * sine
    coarse[2] = -sine

    halo_both([0], arrive)
    edge_columns(PAD - 4, 4, end - 4, 4)

    def sum_copy(s, d):
        return pltpu.make_async_remote_copy(
            src_ref=part.at[s],
            dst_ref=slots.at[s, d],
            send_sem=sum_s.at[s, d],
            recv_sem=sum_r.at[s, d],
            device_id={"tile": lax.rem(me + d, tiles)},
            device_id_type=MESH,
        )

    half = lax.broadcasted_iota(jnp.int32, (1, LANE), 1) < LANE // 2

    def phi_of(s):
        return x.at[0] if s == 0 else later.at[s - 1, 0]

    def elev_of(s):
        return x.at[2] if s == 0 else later.at[s - 1, 1]

    def inner_products(s):
        phi = phi_of(s)
        for a in wide:
            res[:, a : a + SUB] = 4.0 * rows8(phi, a) - neighbours(phi, a)
        gram = [None] * 9

        def add(k, v):
            gram[k] = v if gram[k] is None else gram[k] + v

        for a in wide:
            r = rows8(res, a)
            for m in range(LEVELS):
                c[m, 0, :, a : a + SUB] = rows8(dw.at[m], a) * r
        for i in range(2):
            for m in range(LEVELS):
                for a in wide:
                    v = neighbours(c.at[m, i], a)
                    u[m, i, :, a : a + SUB] = v
                    c[m, i + 1, :, a : a + SUB] = rows8(dm.at[m], a) * v
        for m in range(LEVELS):
            for a in own:
                us = [rows8(res, a), rows8(u.at[m, 0], a), rows8(u.at[m, 1], a), neighbours(c.at[m, 2], a)]
                k = 0
                for i in range(4):
                    for j in range(max(i, 1), 4):
                        v = jnp.sum(us[i] * us[j], axis=0)
                        add(k, WEIGHT[m] * v if i == 0 else v)
                        k += 1
                for i in range(3):
                    if m == 0:
                        planes[i, :, a : a + SUB] = us[i + 1]
                    else:
                        planes[i, :, a : a + SUB] += us[i + 1]
        gram = [4.0 * g for g in gram]
        square = None
        for a in own:
            bottom = [rows8(res, a)] + [rows8(planes.at[i], a) for i in range(3)]
            k = 0
            for i in range(4):
                for j in range(max(i, 1), 4):
                    gram[k] = gram[k] + 0.5 * jnp.sum(bottom[i] * bottom[j], axis=0)
                    k += 1
            v = jnp.sum(bottom[0] * bottom[0], axis=0)
            square = v if square is None else square + v
        gram = [jnp.sum(g, axis=0, keepdims=True) for g in [LEVELS * square] + gram]
        for k in range(FOLD):
            a, b = gram[k], gram[k + FOLD]
            part[s, k : k + 1] = jnp.where(half, a, b) + pltpu.roll(
                jnp.where(half, b, a), LANE // 2, axis=1
            )

    def own_tops():
        for a in own:
            for i in range(3):
                y = None
                for m in range(LEVELS):
                    v = TOPROW[m] * rows8(c.at[m, i], a)
                    y = v if y is None else y + v
                top[i, :, a : a + SUB] = y

    def beyond(s, regions):
        phi = phi_of(s)
        for side, (_, first_rows, second_row, _) in enumerate(regions):
            base = second_row - SUB
            for a in first_rows:
                r = 4.0 * rows8(phi, a) - neighbours(phi, a)
                for m in range(LEVELS):
                    out_c[m, side, 0, :, a - base : a - base + SUB] = rows8(dw.at[m], a) * r
        for m in range(LEVELS):
            for side, (_, _, second_row, _) in enumerate(regions):
                out_c[m, side, 1, :, SUB : 2 * SUB] = rows8(dm.at[m], second_row) * neighbours(
                    out_c.at[m, side, 0], SUB
                )
        for side, (_, _, second_row, third_row) in enumerate(regions):
            at = third_row - second_row + SUB
            ys = [None] * 3
            for m in range(LEVELS):
                c0, c1 = out_c.at[m, side, 0], out_c.at[m, side, 1]
                c2 = rows8(dm.at[m], third_row) * neighbours(c1, at)
                for i, v in enumerate([rows8(c0, at), rows8(c1, at), c2]):
                    v = TOPROW[m] * v
                    ys[i] = v if ys[i] is None else ys[i] + v
            for i in range(3):
                out_y[side, i] = ys[i]

    def explicit(s, a):
        elev, phi = elev_of(s), phi_of(s)
        before_h, after_h = rolled(rows8(elev, a))
        before_f, after_f = rolled(rows8(phi, a))
        he = 0.5 * (rows8(elev, a + 1) - rows8(elev, a - 1))
        fe = 0.5 * (rows8(phi, a + 1) - rows8(phi, a - 1))
        hn = 0.5 * (after_h - before_h)
        fn = 0.5 * (after_f - before_f)
        slope = 1.0 + he * he + hn * hn
        rate_h = SHIP_SPEED * he - (he * fe + hn * fn)
        rate_f = SHIP_SPEED * fe - rows8(elev, a) - 0.5 * (fe * fe + fn * fn) - rows8(x.at[3], a)
        return slope, rate_h, rate_f

    def rates(beta, y, known, a):
        slope, rate_h, rate_f = known
        w = (beta[0] * y[0] + beta[1] * y[1] + beta[2] * y[2]) * rows8(wfac, a)
        ws = w * slope
        return rate_h + ws, rate_f + 0.5 * w * ws

    def advance(s, a, rate_h, rate_f, there=None):
        ahead = TIME_STEP if s == STAGES - 2 else 0.5 * TIME_STEP
        new_f = rows8(x.at[0], a) + ahead * rate_f
        new_h = rows8(x.at[2], a) + ahead * rate_h
        if there is not None:
            new_f = jnp.where(there, new_f, 0.0)
            new_h = jnp.where(there, new_h, 0.0)
        later[s, 0, :, a : a + SUB] = new_f
        later[s, 1, :, a : a + SUB] = new_h

    near = [
        (has_lo, [PAD - 6], PAD - 6, PAD - 4),
        (has_hi, [end - 2], end - 2, end - 4),
    ]
    far = {
        0: [
            (has_lo, [PAD - 12, PAD - 10], PAD - 11, PAD - 12),
            (has_hi, [end + 2, end + 4], end + 3, end + 4),
        ],
        1: [
            (has_lo, [PAD - 10], PAD - 10, PAD - 12),
            (has_hi, [end + 2], end + 2, end + 4),
        ],
    }
    betas = []

    for s in range(STAGES):
        inner_products(s)
        for d in range(1, tiles):
            sum_copy(s, d).start()
        own_tops()
        known = [explicit(s, a) for a in own] if s > 0 else None
        if s == 0:
            halo_both(FAR_PARTS, start)
            halo_both(NEAR_PARTS, arrive)
            edge_columns(PAD - 7, 7, end - 1, 1)
            known = [explicit(s, a) for a in own]
        if s == 1:
            halo_both(FAR_PARTS, arrive)
            edge_columns(PAD - 13, SUB, end + 5, 0)
        if s - 1 in far:
            beyond(s - 1, far[s - 1])
            for side, (there, _, _, third_row) in enumerate(far[s - 1]):
                y = [out_y[side, i] for i in range(3)]
                seen = explicit(s - 1, third_row)
                rate_h, rate_f = rates(betas[s - 1], y, seen, third_row)
                advance(s - 1, third_row, rate_h, rate_f, there)
        if s < STAGES - 1:
            beyond(s, near)
            known_near = [explicit(s, third_row) for _, _, _, third_row in near]

        for d in range(1, tiles):
            sum_copy(s, d).wait_recv()
        whole = part[s]
        for d in range(1, tiles):
            whole = whole + slots[s, d]
        low = jnp.sum(jnp.where(half, whole, 0.0), axis=1, keepdims=True)
        high = jnp.sum(jnp.where(half, 0.0, whole), axis=1, keepdims=True)
        sums = [low[k : k + 1] for k in range(FOLD)] + [high[k : k + 1] for k in range(FOLD)]
        betas.append([jnp.broadcast_to(b, (SUB, LANE)) for b in step_sizes(sums)])

        if s < STAGES - 1:
            for side, (there, _, _, third_row) in enumerate(near):
                y = [out_y[side, i] for i in range(3)]
                rate_h, rate_f = rates(betas[s], y, known_near[side], third_row)
                advance(s, third_row, rate_h, rate_f, there)
        share = (1.0 if s in (0, STAGES - 1) else 2.0) * (TIME_STEP / 6.0)
        for a, seen in zip(own, known):
            y = [rows8(top.at[i], a) for i in range(3)]
            rate_h, rate_f = rates(betas[s], y, seen, a)
            if s < STAGES - 1:
                advance(s, a, rate_h, rate_f)
            b = a - PAD
            if s == 0:
                total[0, :, b : b + SUB] = rows8(x.at[2], a) + share * rate_h
                total[1, :, b : b + SUB] = rows8(x.at[0], a) + share * rate_f
            else:
                total[0, :, b : b + SUB] += share * rate_h
                total[1, :, b : b + SUB] += share * rate_f

    chunk = 2
    pieces = list(range(0, blocks, chunk))

    def chain_copy(k):
        return pltpu.make_async_remote_copy(
            src_ref=chain.at[pl.ds(pieces[k], chunk)],
            dst_ref=chain_in.at[pl.ds(pieces[k], chunk)],
            send_sem=chain_s.at[k],
            recv_sem=chain_r.at[k],
            device_id={"cuts": cut + 1},
            device_id_type=MESH,
        )

    @pl.when(has_prev)
    def _():
        e = x[2, :, PAD:end]
        p = x[0, :, PAD:end]
        total[0] = total[0] - (coarse[0] * e + coarse[1] * p)
        total[1] = total[1] - (coarse[2] * e + coarse[0] * p)

    for k, first in enumerate(pieces):
        span = slice(first, first + chunk)

        @pl.when(has_prev)
        def _():
            chain_copy(k).wait_recv()
            e = chain_in[span, 0]
            p = chain_in[span, 1]
            chain[span, 0] = coarse[0, span] * e + coarse[1, span] * p + total[0, span]
            chain[span, 1] = coarse[2, span] * e + coarse[0, span] * p + total[1, span]

        @pl.when(jnp.logical_not(has_prev))
        def _():
            chain[span, 0] = total[0, span]
            chain[span, 1] = total[1, span]

        @pl.when(has_next)
        def _():
            chain_copy(k).start()

    for j in range(blocks):
        for k in range(2):
            out_ref[0, k, :, j * LANE : (j + 1) * LANE] = chain[j, k]

    halo_both(range(len(PARTS)), leave)

    @pl.when(has_next)
    def _():
        for k in range(len(pieces)):
            chain_copy(k).wait_send()

    for s in range(STAGES):
        for d in range(1, tiles):
            sum_copy(s, d).wait_send()


def local(tiles, slices, state_in, sea_depth, pressure):
    rows, columns = sea_depth.shape
    blocks = columns // LANE
    field = (blocks, rows + 2 * PAD, LANE)
    plane = (blocks, rows, LANE)
    f32 = jnp.float32
    pieces = blocks // 2
    return pl.pallas_call(
        functools.partial(kernel, tiles, slices, rows),
        out_shape=jax.ShapeDtypeStruct(state_in.shape, f32),
        in_specs=[pl.BlockSpec(memory_space=pltpu.HBM)] * 3,
        out_specs=pl.BlockSpec(memory_space=pltpu.VMEM),
        scratch_shapes=[
            pltpu.VMEM(state_in.shape[1:], f32),
            pltpu.VMEM(sea_depth.shape, f32),
            pltpu.VMEM(pressure.shape, f32),
            pltpu.VMEM((4,) + field, f32),
            pltpu.VMEM((STAGES - 1, 2) + field, f32),
            pltpu.VMEM((LEVELS,) + field, f32),
            pltpu.VMEM((LEVELS,) + field, f32),
            pltpu.VMEM(field, f32),
            pltpu.VMEM((3,) + plane, f32),
            pltpu.VMEM((2,) + plane, f32),
            pltpu.VMEM(field, f32),
            pltpu.VMEM((LEVELS, 3) + field, f32),
            pltpu.VMEM((LEVELS, 2) + field, f32),
            pltpu.VMEM((3,) + field, f32),
            pltpu.VMEM((3,) + field, f32),
            pltpu.VMEM((LEVELS, 2, 2, blocks, SPAN, LANE), f32),
            pltpu.VMEM((2, 3, blocks, SUB, LANE), f32),
            pltpu.VMEM((STAGES, FOLD, LANE), f32),
            pltpu.VMEM((STAGES, tiles, FOLD, LANE), f32),
            pltpu.VMEM((blocks, 2, rows, LANE), f32),
            pltpu.VMEM((blocks, 2, rows, LANE), f32),
            pltpu.SemaphoreType.DMA((3,)),
            pltpu.SemaphoreType.DMA((len(PARTS), 2)),
            pltpu.SemaphoreType.DMA((len(PARTS), 2)),
            pltpu.SemaphoreType.DMA((STAGES, tiles)),
            pltpu.SemaphoreType.DMA((STAGES, tiles)),
            pltpu.SemaphoreType.DMA((pieces,)),
            pltpu.SemaphoreType.DMA((pieces,)),
        ],
        compiler_params=pltpu.CompilerParams(
            collective_id=0, has_side_effects=True, vmem_limit_bytes=60 * 1024 * 1024
        ),
        name="wake_step",
    )(state_in, sea_depth, pressure)


def solution(mesh):
    placed = (P("cuts", None, "tile", None), P("tile", None), P("tile", None))
    return jax.shard_map(
        functools.partial(local, mesh.shape["tile"], mesh.shape["cuts"]),
        mesh=mesh,
        in_specs=placed,
        out_specs=P("cuts", None, "tile", None),
        check_vma=False,
    )
```

```python
import functools
import math

import jax
import jax.numpy as jnp
from jax import lax
from jax.experimental import pallas as pl
from jax.experimental.pallas import tpu as pltpu
from jax.sharding import PartitionSpec as P

LEVELS = 8
STAGES = 4
TIME_STEP = 0.8
SHIP_SPEED = 0.5
EPSILON = 1e-06
MESH = pl.DeviceIdType.MESH
SUB = 8
LANE = 128
FOLD = 5
PAD = 16
SPAN = 24
PARTS = [(0, 2, 0, 4), (0, 2, 4, 3), (2, 2, 0, 5), (0, 2, 7, 6), (2, 2, 5, 6)]
NEAR_PARTS = [1, 2]
FAR_PARTS = [3, 4]

THETA = [(m + 0.5) * math.pi / LEVELS for m in range(LEVELS)]
LAM = [2.0 * math.cos(t) - 2.0 for t in THETA]
WEIGHT = [(-1.0) ** m / math.tan(t / 2) / LEVELS for m, t in enumerate(THETA)]
TOPROW = [math.cos((LEVELS - 2) * t) - 4.0 * math.cos((LEVELS - 1) * t) for t in THETA]


def rolled(v):
    lane = lax.broadcasted_iota(jnp.int32, (1,) + v.shape[1:], 2)
    r = pltpu.roll(v, 1, axis=2)
    l = pltpu.roll(v, LANE - 1, axis=2)
    zero = jnp.zeros_like(v[:1])
    before = jnp.where(lane == 0, jnp.concatenate([zero, r[:-1]], axis=0), r)
    after = jnp.where(lane == LANE - 1, jnp.concatenate([l[1:], zero], axis=0), l)
    return before, after


def rows8(ref, a):
    return ref[:, a : a + SUB]


def neighbours(ref, a):
    before, after = rolled(rows8(ref, a))
    return (rows8(ref, a + 1) + rows8(ref, a - 1)) + (before + after)


def step_sizes(g):
    g00, g01, g02, g03, g11, g12, g13, g22, g23, g33 = g
    gram = [[g00, g01, g02, g03], [g01, g11, g12, g13], [g02, g12, g22, g23], [g03, g13, g23, g33]]

    def quad(c, left, right):
        total = None
        for i, ci in enumerate(c):
            for j, cj in enumerate(c):
                if left == right and j < i:
                    continue
                term = ci * cj * gram[i + left][j + right]
                if left == right and j > i:
                    term = 2.0 * term
                total = term if total is None else total + term
        return total

    coef = [jnp.ones_like(g00)]
    beta = [0.0, 0.0, 0.0]
    for sweep in range(3):
        rr = quad(coef, 0, 0)
        re = quad(coef, 0, 1)
        ee = quad(coef, 1, 1)
        inv = 1.0 / (jnp.maximum(rr + 2.0 * re + ee, 0.0) + EPSILON)
        s = (rr + re) * inv
        t = (re + ee + EPSILON) * inv
        for j, c in enumerate(coef):
            beta[j] = beta[j] + s * c
        nxt = [t * c for c in coef] + [jnp.zeros_like(s)]
        for j, c in enumerate(coef):
            nxt[j + 1] = nxt[j + 1] - s * c
        coef = nxt
    return beta


def meetings(tiles):
    bits = [1 << k for k in range((tiles - 1).bit_length())]
    known = {0, *bits}
    rounds = []
    while True:
        few = known | {1 ^ v for v in known}
        those = [1] if rounds and len(few) == tiles else bits
        known = known | {b ^ v for b in those for v in known}
        rounds.append(those)
        if len(known) == tiles:
            return rounds


def kernel(
    tiles, slices, rows, state_ref, depth_ref, press_ref, out_ref,
    raw, raw_d, raw_p, x, later, dm, dw, wfac, coarse, total, res, c, u, planes, top, out_c, out_y,
    part, slots, chain, chain_in,
    load_s, halo_s, halo_r, sum_s, sum_r, chain_s, chain_r, ready,
):
    me = lax.axis_index("tile")
    cut = lax.axis_index("cuts")
    has_lo = me > 0
    has_hi = me < tiles - 1
    has_prev = cut > 0
    has_next = cut < slices - 1
    blocks = x.shape[1]
    end = PAD + rows
    own = list(range(PAD, end, SUB))
    wide = list(range(PAD - 3, end - 5, SUB)) + [end - 5]
    wide = sorted(set(wide))

    loads = [
        pltpu.make_async_copy(state_ref.at[0], raw, load_s.at[0]),
        pltpu.make_async_copy(depth_ref, raw_d, load_s.at[1]),
        pltpu.make_async_copy(press_ref, raw_p, load_s.at[2]),
    ]
    for load in loads:
        load.start()

    for p in range(4):
        x[p, :, 0:PAD] = jnp.zeros((blocks, PAD, LANE), jnp.float32)
        x[p, :, end : end + PAD] = jnp.zeros((blocks, PAD, LANE), jnp.float32)

    barrier = pltpu.get_barrier_semaphore()
    cross = me + 2 * lax.rem(me, 2) - 1
    has_cross = (cross >= 0) & (cross < tiles)

    def partner(bit):
        return me + bit * (1 - 2 * lax.rem(me // bit, 2))

    def tell(sem, bits):
        for bit in bits:
            pl.semaphore_signal(sem, inc=1, device_id={"tile": partner(bit)}, device_id_type=MESH)

    bits = [1 << k for k in range((tiles - 1).bit_length())]
    tell(barrier, bits)

    @pl.when(has_cross)
    def _():
        pl.semaphore_signal(barrier, inc=1, device_id={"tile": cross}, device_id_type=MESH)

    @pl.when(has_prev)
    def _():
        pl.semaphore_signal(barrier, inc=1, device_id={"cuts": cut - 1}, device_id_type=MESH)

    @pl.when(has_next)
    def _():
        pl.semaphore_signal(barrier, inc=1, device_id={"cuts": cut + 1}, device_id_type=MESH)

    for load in loads:
        load.wait()
    for j in range(blocks):
        cols = slice(j * LANE, (j + 1) * LANE)
        x[0, j, PAD:end] = raw[1, :, cols]
        x[1, j, PAD:end] = raw_d[:, cols]
        x[2, j, PAD:end] = raw[0, :, cols]
        x[3, j, PAD:end] = raw_p[:, cols]

    def halo_copy(k, side):
        p, count, a, size = PARTS[k]
        if side == 0:
            src, dst = PAD + a, end + a
        else:
            src, dst = end - a - size, PAD - a - size
        return pltpu.make_async_remote_copy(
            src_ref=x.at[pl.ds(p, count), :, pl.ds(src, size)],
            dst_ref=x.at[pl.ds(p, count), :, pl.ds(dst, size)],
            send_sem=halo_s.at[k, side],
            recv_sem=halo_r.at[k, side],
            device_id={"tile": me - 1 if side == 0 else me + 1},
            device_id_type=MESH,
        )

    def halo_both(ks, act):
        @pl.when(has_lo)
        def _():
            for k in ks:
                act(k, 0)

        @pl.when(has_hi)
        def _():
            for k in ks:
                act(k, 1)

    start = lambda k, side: halo_copy(k, side).start()
    arrive = lambda k, side: halo_copy(k, 1 - side).wait_recv()
    leave = lambda k, side: halo_copy(k, side).wait_send()

    def columns(a, inside=None):
        safe = rows8(x.at[1], a)
        if inside is not None:
            safe = jnp.where(inside, safe, 1.0)
        inv_depth = 1.0 / safe
        vert = LEVELS * inv_depth
        vert = vert * vert
        for m in range(LEVELS):
            inverse = 1.0 / (vert * LAM[m] - 4.0)
            if inside is not None:
                inverse = jnp.where(inside, inverse, 0.0)
            dm[m, :, a : a + SUB] = inverse
            dw[m, :, a : a + SUB] = WEIGHT[m] * inverse
        wfac[:, a : a + SUB] = (0.5 * LEVELS) * inv_depth

    sub = lax.broadcasted_iota(jnp.int32, (1, SUB, LANE), 1)

    def edge_columns(a_lo, own_lo, a_hi, own_hi):
        columns(a_lo, sub + SUB * has_lo.astype(jnp.int32) >= own_lo)
        columns(a_hi, sub - SUB * has_hi.astype(jnp.int32) < own_hi)

    for a in own:
        columns(a)

    pl.semaphore_wait(
        barrier,
        len(bits)
        + has_cross.astype(jnp.int32)
        + has_prev.astype(jnp.int32)
        + has_next.astype(jnp.int32),
    )
    rounds = meetings(tiles)
    for k, those in enumerate(rounds):
        tell(ready.at[k], those)
        if k == 0:
            halo_both([0], start)
        if k < len(rounds) - 1:
            pl.semaphore_wait(ready.at[k], len(those))
    halo_both(NEAR_PARTS, start)

    depth = x[1, :, PAD:end]
    stiff = jnp.tanh(depth)
    z = TIME_STEP * TIME_STEP * stiff
    coarse[0] = 1.0 + z * (-1 / 2 + z * (1 / 24 + z * (-1 / 720 + z * (1 / 40320 - z / 3628800))))
    sine = TIME_STEP * (
        1.0 + z * (-1 / 6 + z * (1 / 120 + z * (-1 / 5040 + z * (1 / 362880 - z / 39916800))))
    )
    coarse[1] = stiff * sine
    coarse[2] = -sine

    halo_both([0], arrive)
    edge_columns(PAD - 4, 4, end - 4, 4)

    def sum_copy(s, d):
        return pltpu.make_async_remote_copy(
            src_ref=part.at[s],
            dst_ref=slots.at[s, d],
            send_sem=sum_s.at[s, d],
            recv_sem=sum_r.at[s, d],
            device_id={"tile": lax.rem(me + d, tiles)},
            device_id_type=MESH,
        )

    half = lax.broadcasted_iota(jnp.int32, (1, LANE), 1) < LANE // 2

    def phi_of(s):
        return x.at[0] if s == 0 else later.at[s - 1, 0]

    def elev_of(s):
        return x.at[2] if s == 0 else later.at[s - 1, 1]

    def inner_products(s):
        phi = phi_of(s)
        for a in wide:
            res[:, a : a + SUB] = 4.0 * rows8(phi, a) - neighbours(phi, a)
        gram = [None] * 9

        def add(k, v):
            gram[k] = v if gram[k] is None else gram[k] + v

        for a in wide:
            r = rows8(res, a)
            for m in range(LEVELS):
                c[m, 0, :, a : a + SUB] = rows8(dw.at[m], a) * r
        for i in range(2):
            for m in range(LEVELS):
                for a in wide:
                    v = neighbours(c.at[m, i], a)
                    u[m, i, :, a : a + SUB] = v
                    c[m, i + 1, :, a : a + SUB] = rows8(dm.at[m], a) * v
        for m in range(LEVELS):
            for a in own:
                us = [rows8(res, a), rows8(u.at[m, 0], a), rows8(u.at[m, 1], a), neighbours(c.at[m, 2], a)]
                k = 0
                for i in range(4):
                    for j in range(max(i, 1), 4):
                        v = jnp.sum(us[i] * us[j], axis=0)
                        add(k, WEIGHT[m] * v if i == 0 else v)
                        k += 1
                for i in range(3):
                    if m == 0:
                        planes[i, :, a : a + SUB] = us[i + 1]
                    else:
                        planes[i, :, a : a + SUB] += us[i + 1]
        gram = [4.0 * g for g in gram]
        square = None
        for a in own:
            bottom = [rows8(res, a)] + [rows8(planes.at[i], a) for i in range(3)]
            k = 0
            for i in range(4):
                for j in range(max(i, 1), 4):
                    gram[k] = gram[k] + 0.5 * jnp.sum(bottom[i] * bottom[j], axis=0)
                    k += 1
            v = jnp.sum(bottom[0] * bottom[0], axis=0)
            square = v if square is None else square + v
        gram = [jnp.sum(g, axis=0, keepdims=True) for g in [LEVELS * square] + gram]
        for k in range(FOLD):
            a, b = gram[k], gram[k + FOLD]
            part[s, k : k + 1] = jnp.where(half, a, b) + pltpu.roll(
                jnp.where(half, b, a), LANE // 2, axis=1
            )

    def own_tops():
        for a in own:
            for i in range(3):
                y = None
                for m in range(LEVELS):
                    v = TOPROW[m] * rows8(c.at[m, i], a)
                    y = v if y is None else y + v
                top[i, :, a : a + SUB] = y

    def beyond(s, regions):
        phi = phi_of(s)
        for side, (_, first_rows, second_row, _) in enumerate(regions):
            base = second_row - SUB
            for a in first_rows:
                r = 4.0 * rows8(phi, a) - neighbours(phi, a)
                for m in range(LEVELS):
                    out_c[m, side, 0, :, a - base : a - base + SUB] = rows8(dw.at[m], a) * r
        for m in range(LEVELS):
            for side, (_, _, second_row, _) in enumerate(regions):
                out_c[m, side, 1, :, SUB : 2 * SUB] = rows8(dm.at[m], second_row) * neighbours(
                    out_c.at[m, side, 0], SUB
                )
        for side, (_, _, second_row, third_row) in enumerate(regions):
            at = third_row - second_row + SUB
            ys = [None] * 3
            for m in range(LEVELS):
                c0, c1 = out_c.at[m, side, 0], out_c.at[m, side, 1]
                c2 = rows8(dm.at[m], third_row) * neighbours(c1, at)
                for i, v in enumerate([rows8(c0, at), rows8(c1, at), c2]):
                    v = TOPROW[m] * v
                    ys[i] = v if ys[i] is None else ys[i] + v
            for i in range(3):
                out_y[side, i] = ys[i]

    def explicit(s, a):
        elev, phi = elev_of(s), phi_of(s)
        before_h, after_h = rolled(rows8(elev, a))
        before_f, after_f = rolled(rows8(phi, a))
        he = 0.5 * (rows8(elev, a + 1) - rows8(elev, a - 1))
        fe = 0.5 * (rows8(phi, a + 1) - rows8(phi, a - 1))
        hn = 0.5 * (after_h - before_h)
        fn = 0.5 * (after_f - before_f)
        slope = 1.0 + he * he + hn * hn
        rate_h = SHIP_SPEED * he - (he * fe + hn * fn)
        rate_f = SHIP_SPEED * fe - rows8(elev, a) - 0.5 * (fe * fe + fn * fn) - rows8(x.at[3], a)
        return slope, rate_h, rate_f

    def rates(beta, y, known, a):
        slope, rate_h, rate_f = known
        w = (beta[0] * y[0] + beta[1] * y[1] + beta[2] * y[2]) * rows8(wfac, a)
        ws = w * slope
        return rate_h + ws, rate_f + 0.5 * w * ws

    def advance(s, a, rate_h, rate_f, there=None):
        ahead = TIME_STEP if s == STAGES - 2 else 0.5 * TIME_STEP
        new_f = rows8(x.at[0], a) + ahead * rate_f
        new_h = rows8(x.at[2], a) + ahead * rate_h
        if there is not None:
            new_f = jnp.where(there, new_f, 0.0)
            new_h = jnp.where(there, new_h, 0.0)
        later[s, 0, :, a : a + SUB] = new_f
        later[s, 1, :, a : a + SUB] = new_h

    near = [
        (has_lo, [PAD - 6], PAD - 6, PAD - 4),
        (has_hi, [end - 2], end - 2, end - 4),
    ]
    far = {
        0: [
            (has_lo, [PAD - 12, PAD - 10], PAD - 11, PAD - 12),
            (has_hi, [end + 2, end + 4], end + 3, end + 4),
        ],
        1: [
            (has_lo, [PAD - 10], PAD - 10, PAD - 12),
            (has_hi, [end + 2], end + 2, end + 4),
        ],
    }
    betas = []

    for s in range(STAGES):
        inner_products(s)
        if s == 0:
            pl.semaphore_wait(ready.at[len(rounds) - 1], len(rounds[-1]))
        for d in range(1, tiles):
            sum_copy(s, d).start()
        own_tops()
        known = [explicit(s, a) for a in own] if s > 0 else None
        if s == 0:
            halo_both(FAR_PARTS, start)
            halo_both(NEAR_PARTS, arrive)
            edge_columns(PAD - 7, 7, end - 1, 1)
            known = [explicit(s, a) for a in own]
        if s == 1:
            halo_both(FAR_PARTS, arrive)
            edge_columns(PAD - 13, SUB, end + 5, 0)
        if s - 1 in far:
            beyond(s - 1, far[s - 1])
            for side, (there, _, _, third_row) in enumerate(far[s - 1]):
                y = [out_y[side, i] for i in range(3)]
                seen = explicit(s - 1, third_row)
                rate_h, rate_f = rates(betas[s - 1], y, seen, third_row)
                advance(s - 1, third_row, rate_h, rate_f, there)
        if s < STAGES - 1:
            beyond(s, near)
            known_near = [explicit(s, third_row) for _, _, _, third_row in near]

        for d in range(1, tiles):
            sum_copy(s, d).wait_recv()
        whole = part[s]
        for d in range(1, tiles):
            whole = whole + slots[s, d]
        low = jnp.sum(jnp.where(half, whole, 0.0), axis=1, keepdims=True)
        high = jnp.sum(jnp.where(half, 0.0, whole), axis=1, keepdims=True)
        sums = [low[k : k + 1] for k in range(FOLD)] + [high[k : k + 1] for k in range(FOLD)]
        betas.append([jnp.broadcast_to(b, (SUB, LANE)) for b in step_sizes(sums)])

        if s < STAGES - 1:
            for side, (there, _, _, third_row) in enumerate(near):
                y = [out_y[side, i] for i in range(3)]
                rate_h, rate_f = rates(betas[s], y, known_near[side], third_row)
                advance(s, third_row, rate_h, rate_f, there)
        share = (1.0 if s in (0, STAGES - 1) else 2.0) * (TIME_STEP / 6.0)
        for a, seen in zip(own, known):
            y = [rows8(top.at[i], a) for i in range(3)]
            rate_h, rate_f = rates(betas[s], y, seen, a)
            if s < STAGES - 1:
                advance(s, a, rate_h, rate_f)
            b = a - PAD
            if s == 0:
                total[0, :, b : b + SUB] = rows8(x.at[2], a) + share * rate_h
                total[1, :, b : b + SUB] = rows8(x.at[0], a) + share * rate_f
            else:
                total[0, :, b : b + SUB] += share * rate_h
                total[1, :, b : b + SUB] += share * rate_f

    chunk = 2
    pieces = list(range(0, blocks, chunk))

    def chain_copy(k):
        return pltpu.make_async_remote_copy(
            src_ref=chain.at[pl.ds(pieces[k], chunk)],
            dst_ref=chain_in.at[pl.ds(pieces[k], chunk)],
            send_sem=chain_s.at[k],
            recv_sem=chain_r.at[k],
            device_id={"cuts": cut + 1},
            device_id_type=MESH,
        )

    @pl.when(has_prev)
    def _():
        e = x[2, :, PAD:end]
        p = x[0, :, PAD:end]
        total[0] = total[0] - (coarse[0] * e + coarse[1] * p)
        total[1] = total[1] - (coarse[2] * e + coarse[0] * p)

    for k, first in enumerate(pieces):
        span = slice(first, first + chunk)

        @pl.when(has_prev)
        def _():
            chain_copy(k).wait_recv()
            e = chain_in[span, 0]
            p = chain_in[span, 1]
            chain[span, 0] = coarse[0, span] * e + coarse[1, span] * p + total[0, span]
            chain[span, 1] = coarse[2, span] * e + coarse[0, span] * p + total[1, span]

        @pl.when(jnp.logical_not(has_prev))
        def _():
            chain[span, 0] = total[0, span]
            chain[span, 1] = total[1, span]

        @pl.when(has_next)
        def _():
            chain_copy(k).start()

    for j in range(blocks):
        for k in range(2):
            out_ref[0, k, :, j * LANE : (j + 1) * LANE] = chain[j, k]

    halo_both(range(len(PARTS)), leave)

    @pl.when(has_next)
    def _():
        for k in range(len(pieces)):
            chain_copy(k).wait_send()

    for s in range(STAGES):
        for d in range(1, tiles):
            sum_copy(s, d).wait_send()


def local(tiles, slices, state_in, sea_depth, pressure):
    rows, columns = sea_depth.shape
    blocks = columns // LANE
    field = (blocks, rows + 2 * PAD, LANE)
    plane = (blocks, rows, LANE)
    f32 = jnp.float32
    pieces = blocks // 2
    return pl.pallas_call(
        functools.partial(kernel, tiles, slices, rows),
        out_shape=jax.ShapeDtypeStruct(state_in.shape, f32),
        in_specs=[pl.BlockSpec(memory_space=pltpu.HBM)] * 3,
        out_specs=pl.BlockSpec(memory_space=pltpu.VMEM),
        scratch_shapes=[
            pltpu.VMEM(state_in.shape[1:], f32),
            pltpu.VMEM(sea_depth.shape, f32),
            pltpu.VMEM(pressure.shape, f32),
            pltpu.VMEM((4,) + field, f32),
            pltpu.VMEM((STAGES - 1, 2) + field, f32),
            pltpu.VMEM((LEVELS,) + field, f32),
            pltpu.VMEM((LEVELS,) + field, f32),
            pltpu.VMEM(field, f32),
            pltpu.VMEM((3,) + plane, f32),
            pltpu.VMEM((2,) + plane, f32),
            pltpu.VMEM(field, f32),
            pltpu.VMEM((LEVELS, 3) + field, f32),
            pltpu.VMEM((LEVELS, 2) + field, f32),
            pltpu.VMEM((3,) + field, f32),
            pltpu.VMEM((3,) + field, f32),
            pltpu.VMEM((LEVELS, 2, 2, blocks, SPAN, LANE), f32),
            pltpu.VMEM((2, 3, blocks, SUB, LANE), f32),
            pltpu.VMEM((STAGES, FOLD, LANE), f32),
            pltpu.VMEM((STAGES, tiles, FOLD, LANE), f32),
            pltpu.VMEM((blocks, 2, rows, LANE), f32),
            pltpu.VMEM((blocks, 2, rows, LANE), f32),
            pltpu.SemaphoreType.DMA((3,)),
            pltpu.SemaphoreType.DMA((len(PARTS), 2)),
            pltpu.SemaphoreType.DMA((len(PARTS), 2)),
            pltpu.SemaphoreType.DMA((STAGES, tiles)),
            pltpu.SemaphoreType.DMA((STAGES, tiles)),
            pltpu.SemaphoreType.DMA((pieces,)),
            pltpu.SemaphoreType.DMA((pieces,)),
            pltpu.SemaphoreType.REGULAR((len(meetings(tiles)),)),
        ],
        compiler_params=pltpu.CompilerParams(
            collective_id=0, has_side_effects=True, vmem_limit_bytes=60 * 1024 * 1024
        ),
        name="wake_step",
    )(state_in, sea_depth, pressure)


def solution(mesh):
    placed = (P("cuts", None, "tile", None), P("tile", None), P("tile", None))
    return jax.shard_map(
        functools.partial(local, mesh.shape["tile"], mesh.shape["cuts"]),
        mesh=mesh,
        in_specs=placed,
        out_specs=P("cuts", None, "tile", None),
        check_vma=False,
    )
```

```python
import functools
import math

import jax
import jax.numpy as jnp
from jax import lax
from jax.experimental import pallas as pl
from jax.experimental.pallas import tpu as pltpu
from jax.sharding import PartitionSpec as P

LEVELS = 8
STAGES = 4
TIME_STEP = 0.8
SHIP_SPEED = 0.5
EPSILON = 1e-06
MESH = pl.DeviceIdType.MESH
SUB = 8
LANE = 128
FOLD = 5
PAD = 16
SPAN = 24
GROUP = 2
PARTS = [(0, 2, 0, 4), (0, 2, 4, 3), (2, 2, 0, 5), (0, 2, 7, 6), (2, 2, 5, 6)]
NEAR_PARTS = [1, 2]
FAR_PARTS = [3, 4]

THETA = [(m + 0.5) * math.pi / LEVELS for m in range(LEVELS)]
LAM = [2.0 * math.cos(t) - 2.0 for t in THETA]
WEIGHT = [(-1.0) ** m / math.tan(t / 2) / LEVELS for m, t in enumerate(THETA)]
TOPROW = [math.cos((LEVELS - 2) * t) - 4.0 * math.cos((LEVELS - 1) * t) for t in THETA]


def rolled(v):
    lane = lax.broadcasted_iota(jnp.int32, (1,) + v.shape[1:], 2)
    r = pltpu.roll(v, 1, axis=2)
    l = pltpu.roll(v, LANE - 1, axis=2)
    zero = jnp.zeros_like(v[:1])
    before = jnp.where(lane == 0, jnp.concatenate([zero, r[:-1]], axis=0), r)
    after = jnp.where(lane == LANE - 1, jnp.concatenate([l[1:], zero], axis=0), l)
    return before, after


def stream(ref, a):
    lane = lax.broadcasted_iota(jnp.int32, (SUB, LANE), 1)
    blocks = ref.shape[0]
    r_old = l_old = r_far = None
    for j in range(blocks + 1):
        if j < blocks:
            v = ref[j, a : a + SUB]
            r = pltpu.roll(v, 1, axis=1)
            l = pltpu.roll(v, LANE - 1, axis=1)
        else:
            l = jnp.zeros((SUB, LANE), jnp.float32)
        if j > 0:
            before = jnp.where(lane == 0, r_far, r_old)
            after = jnp.where(lane == LANE - 1, l, l_old)
            yield j - 1, before, after
        r_far = r_old if j > 0 else jnp.zeros((SUB, LANE), jnp.float32)
        r_old, l_old = r, l


def all_around(ref, a):
    for j, before, after in stream(ref, a):
        yield j, (ref[j, a + 1 : a + 1 + SUB] + ref[j, a - 1 : a - 1 + SUB]) + (before + after)


def rows8(ref, a):
    return ref[:, a : a + SUB]


def neighbours(ref, a):
    before, after = rolled(rows8(ref, a))
    return (rows8(ref, a + 1) + rows8(ref, a - 1)) + (before + after)


def step_sizes(g):
    g00, g01, g02, g03, g11, g12, g13, g22, g23, g33 = g
    gram = [[g00, g01, g02, g03], [g01, g11, g12, g13], [g02, g12, g22, g23], [g03, g13, g23, g33]]

    def quad(c, left, right):
        total = None
        for i, ci in enumerate(c):
            for j, cj in enumerate(c):
                if left == right and j < i:
                    continue
                term = ci * cj * gram[i + left][j + right]
                if left == right and j > i:
                    term = 2.0 * term
                total = term if total is None else total + term
        return total

    coef = [jnp.ones_like(g00)]
    beta = [0.0, 0.0, 0.0]
    for sweep in range(3):
        rr = quad(coef, 0, 0)
        re = quad(coef, 0, 1)
        ee = quad(coef, 1, 1)
        inv = 1.0 / (jnp.maximum(rr + 2.0 * re + ee, 0.0) + EPSILON)
        s = (rr + re) * inv
        t = (re + ee + EPSILON) * inv
        for j, c in enumerate(coef):
            beta[j] = beta[j] + s * c
        nxt = [t * c for c in coef] + [jnp.zeros_like(s)]
        for j, c in enumerate(coef):
            nxt[j + 1] = nxt[j + 1] - s * c
        coef = nxt
    return beta


def meetings(tiles):
    bits = [1 << k for k in range((tiles - 1).bit_length())]
    known = {0, *bits}
    rounds = []
    while True:
        few = known | {1 ^ v for v in known}
        those = [1] if rounds and len(few) == tiles else bits
        known = known | {b ^ v for b in those for v in known}
        rounds.append(those)
        if len(known) == tiles:
            return rounds


def kernel(
    tiles, slices, rows, state_ref, depth_ref, press_ref, out_ref,
    raw, raw_d, raw_p, x, later, dm, dw, dw_before, dw_after, first_top, wfac, coarse, total, res, beside, sides_ref, c, u, top, out_c, out_y,
    part, slots, chain, chain_in,
    load_s, halo_s, halo_r, sum_s, sum_r, chain_s, chain_r, ready,
):
    me = lax.axis_index("tile")
    cut = lax.axis_index("cuts")
    has_lo = me > 0
    has_hi = me < tiles - 1
    has_prev = cut > 0
    has_next = cut < slices - 1
    blocks = x.shape[1]
    end = PAD + rows
    own = list(range(PAD, end, SUB))
    wide = list(range(PAD - 3, end - 5, SUB)) + [end - 5]
    wide = sorted(set(wide))

    loads = [
        pltpu.make_async_copy(state_ref.at[0], raw, load_s.at[0]),
        pltpu.make_async_copy(depth_ref, raw_d, load_s.at[1]),
        pltpu.make_async_copy(press_ref, raw_p, load_s.at[2]),
    ]
    for load in loads:
        load.start()

    barrier = pltpu.get_barrier_semaphore()
    cross = me + 2 * lax.rem(me, 2) - 1
    has_cross = (cross >= 0) & (cross < tiles)

    bits = [1 << k for k in range((tiles - 1).bit_length())]

    def partner(d):
        return me + sum(bit * (1 - 2 * lax.rem(me // bit, 2)) for bit in bits if d & bit)

    def tell(sem, bits):
        for bit in bits:
            pl.semaphore_signal(sem, inc=1, device_id={"tile": partner(bit)}, device_id_type=MESH)

    tell(barrier, bits)

    @pl.when(has_cross)
    def _():
        pl.semaphore_signal(barrier, inc=1, device_id={"tile": cross}, device_id_type=MESH)

    @pl.when(has_prev)
    def _():
        pl.semaphore_signal(barrier, inc=1, device_id={"cuts": cut - 1}, device_id_type=MESH)

    @pl.when(has_next)
    def _():
        pl.semaphore_signal(barrier, inc=1, device_id={"cuts": cut + 1}, device_id_type=MESH)

    for there, a in ((has_lo, 0), (has_hi, end)):

        @pl.when(jnp.logical_not(there))
        def _():
            x[:, :, a : a + PAD] = jnp.zeros((4, blocks, PAD, LANE), jnp.float32)

    for load in loads:
        load.wait()
    for j in range(blocks):
        cols = slice(j * LANE, (j + 1) * LANE)
        x[0, j, PAD:end] = raw[1, :, cols]
        x[1, j, PAD:end] = raw_d[:, cols]
        x[2, j, PAD:end] = raw[0, :, cols]
        x[3, j, PAD:end] = raw_p[:, cols]

    def halo_copy(k, side):
        p, count, a, size = PARTS[k]
        if side == 0:
            src, dst = PAD + a, end + a
        else:
            src, dst = end - a - size, PAD - a - size
        return pltpu.make_async_remote_copy(
            src_ref=x.at[pl.ds(p, count), :, pl.ds(src, size)],
            dst_ref=x.at[pl.ds(p, count), :, pl.ds(dst, size)],
            send_sem=halo_s.at[k, side],
            recv_sem=halo_r.at[k, side],
            device_id={"tile": me - 1 if side == 0 else me + 1},
            device_id_type=MESH,
        )

    def halo_both(ks, act):
        @pl.when(has_lo)
        def _():
            for k in ks:
                act(k, 0)

        @pl.when(has_hi)
        def _():
            for k in ks:
                act(k, 1)

    start = lambda k, side: halo_copy(k, side).start()
    arrive = lambda k, side: halo_copy(k, 1 - side).wait_recv()
    leave = lambda k, side: halo_copy(k, side).wait_send()

    def columns(a, inside=None):
        safe = rows8(x.at[1], a)
        if inside is not None:
            safe = jnp.where(inside, safe, 1.0)
        inv_depth = 1.0 / safe
        vert = LEVELS * inv_depth
        vert = vert * vert
        tops = None
        for m in range(LEVELS):
            inverse = 1.0 / (vert * LAM[m] - 4.0)
            if inside is not None:
                inverse = jnp.where(inside, inverse, 0.0)
            dm[m, :, a : a + SUB] = inverse
            dw[m, :, a : a + SUB] = WEIGHT[m] * inverse
            t = (TOPROW[m] * WEIGHT[m]) * inverse
            tops = t if tops is None else tops + t
        first_top[:, a : a + SUB] = tops
        wfac[:, a : a + SUB] = (0.5 * LEVELS) * inv_depth

    sub = lax.broadcasted_iota(jnp.int32, (1, SUB, LANE), 1)

    def edge_columns(a_lo, own_lo, a_hi, own_hi):
        columns(a_lo, sub + SUB * has_lo.astype(jnp.int32) >= own_lo)
        columns(a_hi, sub - SUB * has_hi.astype(jnp.int32) < own_hi)

    pl.semaphore_wait(
        barrier,
        len(bits)
        + has_cross.astype(jnp.int32)
        + has_prev.astype(jnp.int32)
        + has_next.astype(jnp.int32),
    )
    rounds = meetings(tiles)
    tell(ready.at[0], rounds[0])
    halo_both([0], start)

    for a in own:
        columns(a)
    depth = x[1, :, PAD:end]
    stiff = jnp.tanh(depth)
    z = TIME_STEP * TIME_STEP * stiff
    coarse[0] = 1.0 + z * (-1 / 2 + z * (1 / 24 + z * (-1 / 720 + z * (1 / 40320 - z / 3628800))))
    sine = TIME_STEP * (
        1.0 + z * (-1 / 6 + z * (1 / 120 + z * (-1 / 5040 + z * (1 / 362880 - z / 39916800))))
    )
    coarse[1] = stiff * sine
    coarse[2] = -sine

    for k in range(1, len(rounds)):
        pl.semaphore_wait(ready.at[k - 1], len(rounds[k - 1]))
        tell(ready.at[k], rounds[k])
    halo_both(NEAR_PARTS, start)

    halo_both([0], arrive)
    edge_columns(PAD - 4, 4, end - 4, 4)

    def sum_copy(s, d):
        return pltpu.make_async_remote_copy(
            src_ref=part.at[s],
            dst_ref=slots.at[s, d],
            send_sem=sum_s.at[s, d],
            recv_sem=sum_r.at[s, d],
            device_id={"tile": partner(d)},
            device_id_type=MESH,
        )

    half = lax.broadcasted_iota(jnp.int32, (1, LANE), 1) < LANE // 2

    def phi_of(s):
        return x.at[0] if s == 0 else later.at[s - 1, 0]

    def elev_of(s):
        return x.at[2] if s == 0 else later.at[s - 1, 1]

    def inner_products(s):
        phi = phi_of(s)
        for a in wide:
            res[:, a : a + SUB] = 4.0 * rows8(phi, a) - neighbours(phi, a)
        if s == 0:
            for a in wide:
                r = rows8(res, a)
                for m in range(LEVELS):
                    c[m, 0, :, a : a + SUB] = rows8(dw.at[m], a) * r
        else:
            for a in wide:
                for j, before, after in stream(res, a):
                    beside[0, j, a : a + SUB] = before
                    beside[1, j, a : a + SUB] = after
        gram = [None] * 10

        def add(k, v):
            gram[k] = v if gram[k] is None else gram[k] + v

        def first_power(ms, a, j):
            at, up, down = slice(a, a + SUB), slice(a + 1, a + 1 + SUB), slice(a - 1, a - 1 + SUB)
            r_up, r_down = res[j, up], res[j, down]
            before, after = beside[0, j, at], beside[1, j, at]
            for m in ms:
                v = (dw[m, j, up] * r_up + dw[m, j, down] * r_down) + (
                    dw_before[m, j, at] * before + dw_after[m, j, at] * after
                )
                u[m, 0, j, at] = v
                c[m, 1, j, at] = dm[m, j, at] * v

        def power(i, m, a):
            at = slice(a, a + SUB)
            for j, v in all_around(c.at[m, i], a):
                u[m, i, j, at] = v
                if i < 2:
                    c[m, i + 1, j, at] = dm[m, j, at] * v

        def products(ms, a, j):
            at = slice(a, a + SUB)
            if ms[0] == 0:
                sides = [None] * 6
            else:
                sides = [sides_ref[i, j, at] for i in range(6)]
            for m in ms:
                us = [u[m, i, j, at] for i in range(3)]
                k = 4
                for p in range(3):
                    for q in range(p, 3):
                        add(k, us[p] * us[q])
                        k += 1
                    w = WEIGHT[m] * us[p]
                    sides[p] = us[p] if m == 0 else sides[p] + us[p]
                    sides[3 + p] = w if m == 0 else sides[3 + p] + w
            if ms[-1] < LEVELS - 1:
                for i in range(6):
                    sides_ref[i, j, at] = sides[i]
                return
            u0 = res[j, at]
            add(0, u0 * u0)
            k = 4
            for p in range(3):
                add(1 + p, u0 * (sides[3 + p] + 0.125 * sides[p]))
                part_p = 0.125 * sides[p]
                for q in range(p, 3):
                    add(k, part_p * sides[q])
                    k += 1

        groups = [list(range(m, m + GROUP)) for m in range(0, LEVELS, GROUP)]

        def work(kind, ms):
            if kind == 0 and s > 0:
                return [functools.partial(first_power, ms, a, j) for a in wide for j in range(blocks)]
            if kind < 3:
                windows = own if kind == 2 else wide
                return [functools.partial(power, kind, m, a) for m in ms for a in windows]
            return [functools.partial(products, ms, a, j) for a in own for j in range(blocks)]

        for step in range(len(groups) + 3):
            tasks = []
            for kind in range(4):
                if 0 <= step - kind < len(groups):
                    todo = work(kind, groups[step - kind])
                    tasks += [((n + 0.5) / len(todo), kind, n, task) for n, task in enumerate(todo)]
            for _, _, _, task in sorted(tasks, key=lambda entry: entry[:3]):
                task()
        gram = [LEVELS * gram[0]] + [4.0 * g for g in gram[1:]]
        gram = [jnp.sum(g, axis=0, keepdims=True) for g in gram]
        for k in range(FOLD):
            a, b = gram[k], gram[k + FOLD]
            part[s, k : k + 1] = jnp.where(half, a, b) + pltpu.roll(
                jnp.where(half, b, a), LANE // 2, axis=1
            )

    def own_tops():
        for a in own:
            top[0, :, a : a + SUB] = rows8(first_top, a) * rows8(res, a)
            for i in range(1, 3):
                y = None
                for m in range(LEVELS):
                    v = TOPROW[m] * rows8(c.at[m, i], a)
                    y = v if y is None else y + v
                top[i, :, a : a + SUB] = y

    def beyond(s, regions):
        phi = phi_of(s)
        for side, (_, first_rows, second_row, _) in enumerate(regions):
            base = second_row - SUB
            for a in first_rows:
                r = 4.0 * rows8(phi, a) - neighbours(phi, a)
                for m in range(LEVELS):
                    out_c[m, side, 0, :, a - base : a - base + SUB] = rows8(dw.at[m], a) * r
        for m in range(LEVELS):
            for side, (_, _, second_row, _) in enumerate(regions):
                out_c[m, side, 1, :, SUB : 2 * SUB] = rows8(dm.at[m], second_row) * neighbours(
                    out_c.at[m, side, 0], SUB
                )
        for side, (_, _, second_row, third_row) in enumerate(regions):
            at = third_row - second_row + SUB
            ys = [None] * 3
            for m in range(LEVELS):
                c0, c1 = out_c.at[m, side, 0], out_c.at[m, side, 1]
                c2 = rows8(dm.at[m], third_row) * neighbours(c1, at)
                for i, v in enumerate([rows8(c0, at), rows8(c1, at), c2]):
                    v = TOPROW[m] * v
                    ys[i] = v if ys[i] is None else ys[i] + v
            for i in range(3):
                out_y[side, i] = ys[i]

    def explicit(s, a):
        elev, phi = elev_of(s), phi_of(s)
        before_h, after_h = rolled(rows8(elev, a))
        before_f, after_f = rolled(rows8(phi, a))
        he = 0.5 * (rows8(elev, a + 1) - rows8(elev, a - 1))
        fe = 0.5 * (rows8(phi, a + 1) - rows8(phi, a - 1))
        hn = 0.5 * (after_h - before_h)
        fn = 0.5 * (after_f - before_f)
        slope = 1.0 + he * he + hn * hn
        rate_h = SHIP_SPEED * he - (he * fe + hn * fn)
        rate_f = SHIP_SPEED * fe - rows8(elev, a) - 0.5 * (fe * fe + fn * fn) - rows8(x.at[3], a)
        return slope, rate_h, rate_f

    def rates(beta, y, known, a):
        slope, rate_h, rate_f = known
        w = (beta[0] * y[0] + beta[1] * y[1] + beta[2] * y[2]) * rows8(wfac, a)
        ws = w * slope
        return rate_h + ws, rate_f + 0.5 * w * ws

    def advance(s, a, rate_h, rate_f, there=None):
        ahead = TIME_STEP if s == STAGES - 2 else 0.5 * TIME_STEP
        new_f = rows8(x.at[0], a) + ahead * rate_f
        new_h = rows8(x.at[2], a) + ahead * rate_h
        if there is not None:
            new_f = jnp.where(there, new_f, 0.0)
            new_h = jnp.where(there, new_h, 0.0)
        later[s, 0, :, a : a + SUB] = new_f
        later[s, 1, :, a : a + SUB] = new_h

    near = [
        (has_lo, [PAD - 6], PAD - 6, PAD - 4),
        (has_hi, [end - 2], end - 2, end - 4),
    ]
    far = {
        0: [
            (has_lo, [PAD - 12, PAD - 10], PAD - 11, PAD - 12),
            (has_hi, [end + 2, end + 4], end + 3, end + 4),
        ],
        1: [
            (has_lo, [PAD - 10], PAD - 10, PAD - 12),
            (has_hi, [end + 2], end + 2, end + 4),
        ],
    }
    betas = []

    for s in range(STAGES):
        inner_products(s)
        if s == 0:
            pl.semaphore_wait(ready.at[len(rounds) - 1], len(rounds[-1]))
        for d in range(tiles - 1, 0, -1):
            sum_copy(s, d).start()
        own_tops()
        known = [explicit(s, a) for a in own] if s > 0 else None
        if s == 0:
            halo_both(FAR_PARTS, start)
            halo_both(NEAR_PARTS, arrive)
            edge_columns(PAD - 7, 7, end - 1, 1)
            known = [explicit(s, a) for a in own]
            for m in range(LEVELS):
                for a in wide:
                    before, after = rolled(rows8(dw.at[m], a))
                    dw_before[m, :, a : a + SUB] = before
                    dw_after[m, :, a : a + SUB] = after
        if s == 1:
            halo_both(FAR_PARTS, arrive)
            edge_columns(PAD - 13, SUB, end + 5, 0)
        if s - 1 in far:
            beyond(s - 1, far[s - 1])
            for side, (there, _, _, third_row) in enumerate(far[s - 1]):
                y = [out_y[side, i] for i in range(3)]
                seen = explicit(s - 1, third_row)
                rate_h, rate_f = rates(betas[s - 1], y, seen, third_row)
                advance(s - 1, third_row, rate_h, rate_f, there)
        if s < STAGES - 1:
            beyond(s, near)
            known_near = [explicit(s, third_row) for _, _, _, third_row in near]

        for d in range(1, tiles):
            sum_copy(s, d).wait_recv()
        whole = part[s]
        for d in range(1, tiles):
            whole = whole + slots[s, d]
        low = jnp.sum(jnp.where(half, whole, 0.0), axis=1, keepdims=True)
        high = jnp.sum(jnp.where(half, 0.0, whole), axis=1, keepdims=True)
        sums = [low[k : k + 1] for k in range(FOLD)] + [high[k : k + 1] for k in range(FOLD)]
        betas.append([jnp.broadcast_to(b, (SUB, LANE)) for b in step_sizes(sums)])

        if s < STAGES - 1:
            for side, (there, _, _, third_row) in enumerate(near):
                y = [out_y[side, i] for i in range(3)]
                rate_h, rate_f = rates(betas[s], y, known_near[side], third_row)
                advance(s, third_row, rate_h, rate_f, there)
        share = (1.0 if s in (0, STAGES - 1) else 2.0) * (TIME_STEP / 6.0)
        for a, seen in zip(own, known):
            y = [rows8(top.at[i], a) for i in range(3)]
            rate_h, rate_f = rates(betas[s], y, seen, a)
            if s < STAGES - 1:
                advance(s, a, rate_h, rate_f)
            b = a - PAD
            if s == 0:
                total[0, :, b : b + SUB] = rows8(x.at[2], a) + share * rate_h
                total[1, :, b : b + SUB] = rows8(x.at[0], a) + share * rate_f
            else:
                total[0, :, b : b + SUB] += share * rate_h
                total[1, :, b : b + SUB] += share * rate_f

    chunk = 2
    pieces = list(range(0, blocks, chunk))

    def chain_copy(k):
        return pltpu.make_async_remote_copy(
            src_ref=chain.at[pl.ds(pieces[k], chunk)],
            dst_ref=chain_in.at[pl.ds(pieces[k], chunk)],
            send_sem=chain_s.at[k],
            recv_sem=chain_r.at[k],
            device_id={"cuts": cut + 1},
            device_id_type=MESH,
        )

    @pl.when(has_prev)
    def _():
        e = x[2, :, PAD:end]
        p = x[0, :, PAD:end]
        total[0] = total[0] - (coarse[0] * e + coarse[1] * p)
        total[1] = total[1] - (coarse[2] * e + coarse[0] * p)

    for k, first in enumerate(pieces):
        span = slice(first, first + chunk)

        @pl.when(has_prev)
        def _():
            chain_copy(k).wait_recv()
            e = chain_in[span, 0]
            p = chain_in[span, 1]
            chain[span, 0] = coarse[0, span] * e + coarse[1, span] * p + total[0, span]
            chain[span, 1] = coarse[2, span] * e + coarse[0, span] * p + total[1, span]

        @pl.when(jnp.logical_not(has_prev))
        def _():
            chain[span, 0] = total[0, span]
            chain[span, 1] = total[1, span]

        @pl.when(has_next)
        def _():
            chain_copy(k).start()

    for j in range(blocks):
        for k in range(2):
            out_ref[0, k, :, j * LANE : (j + 1) * LANE] = chain[j, k]

    halo_both(range(len(PARTS)), leave)

    @pl.when(has_next)
    def _():
        for k in range(len(pieces)):
            chain_copy(k).wait_send()

    for s in range(STAGES):
        for d in range(1, tiles):
            sum_copy(s, d).wait_send()


def local(tiles, slices, state_in, sea_depth, pressure):
    rows, columns = sea_depth.shape
    blocks = columns // LANE
    field = (blocks, rows + 2 * PAD, LANE)
    plane = (blocks, rows, LANE)
    f32 = jnp.float32
    pieces = blocks // 2
    return pl.pallas_call(
        functools.partial(kernel, tiles, slices, rows),
        out_shape=jax.ShapeDtypeStruct(state_in.shape, f32),
        in_specs=[pl.BlockSpec(memory_space=pltpu.HBM)] * 3,
        out_specs=pl.BlockSpec(memory_space=pltpu.VMEM),
        scratch_shapes=[
            pltpu.VMEM(state_in.shape[1:], f32),
            pltpu.VMEM(sea_depth.shape, f32),
            pltpu.VMEM(pressure.shape, f32),
            pltpu.VMEM((4,) + field, f32),
            pltpu.VMEM((STAGES - 1, 2) + field, f32),
            pltpu.VMEM((LEVELS,) + field, f32),
            pltpu.VMEM((LEVELS,) + field, f32),
            pltpu.VMEM((LEVELS,) + field, f32),
            pltpu.VMEM((LEVELS,) + field, f32),
            pltpu.VMEM(field, f32),
            pltpu.VMEM(field, f32),
            pltpu.VMEM((3,) + plane, f32),
            pltpu.VMEM((2,) + plane, f32),
            pltpu.VMEM(field, f32),
            pltpu.VMEM((2,) + field, f32),
            pltpu.VMEM((6,) + field, f32),
            pltpu.VMEM((LEVELS, 3) + field, f32),
            pltpu.VMEM((LEVELS, 3) + field, f32),
            pltpu.VMEM((3,) + field, f32),
            pltpu.VMEM((LEVELS, 2, 2, blocks, SPAN, LANE), f32),
            pltpu.VMEM((2, 3, blocks, SUB, LANE), f32),
            pltpu.VMEM((STAGES, FOLD, LANE), f32),
            pltpu.VMEM((STAGES, tiles, FOLD, LANE), f32),
            pltpu.VMEM((blocks, 2, rows, LANE), f32),
            pltpu.VMEM((blocks, 2, rows, LANE), f32),
            pltpu.SemaphoreType.DMA((3,)),
            pltpu.SemaphoreType.DMA((len(PARTS), 2)),
            pltpu.SemaphoreType.DMA((len(PARTS), 2)),
            pltpu.SemaphoreType.DMA((STAGES, tiles)),
            pltpu.SemaphoreType.DMA((STAGES, tiles)),
            pltpu.SemaphoreType.DMA((pieces,)),
            pltpu.SemaphoreType.DMA((pieces,)),
            pltpu.SemaphoreType.REGULAR((len(meetings(tiles)),)),
        ],
        compiler_params=pltpu.CompilerParams(
            collective_id=0, has_side_effects=True, vmem_limit_bytes=60 * 1024 * 1024
        ),
        name="wake_step",
    )(state_in, sea_depth, pressure)


def solution(mesh):
    placed = (P("cuts", None, "tile", None), P("tile", None), P("tile", None))
    return jax.shard_map(
        functools.partial(local, mesh.shape["tile"], mesh.shape["cuts"]),
        mesh=mesh,
        in_specs=placed,
        out_specs=P("cuts", None, "tile", None),
        check_vma=False,
    )
```

```python
import functools
import math

import jax
import jax.numpy as jnp
from jax import lax
from jax.experimental import pallas as pl
from jax.experimental.pallas import tpu as pltpu
from jax.sharding import PartitionSpec as P

LEVELS = 8
STAGES = 4
TIME_STEP = 0.8
SHIP_SPEED = 0.5
EPSILON = 1e-06
MESH = pl.DeviceIdType.MESH
SUB = 8
LANE = 128
FOLD = 5
PAD = 16
SPAN = 24
GROUP = 2
PARTS = [(0, 2, 0, 4), (0, 2, 4, 3), (2, 2, 0, 5), (0, 2, 7, 6), (2, 2, 5, 6)]
NEAR_PARTS = [1, 2]
FAR_PARTS = [3, 4]

THETA = [(m + 0.5) * math.pi / LEVELS for m in range(LEVELS)]
LAM = [2.0 * math.cos(t) - 2.0 for t in THETA]
WEIGHT = [(-1.0) ** m / math.tan(t / 2) / LEVELS for m, t in enumerate(THETA)]
TOPROW = [math.cos((LEVELS - 2) * t) - 4.0 * math.cos((LEVELS - 1) * t) for t in THETA]


def rolled(v):
    lane = lax.broadcasted_iota(jnp.int32, (1,) + v.shape[1:], 2)
    r = pltpu.roll(v, 1, axis=2)
    l = pltpu.roll(v, LANE - 1, axis=2)
    zero = jnp.zeros_like(v[:1])
    before = jnp.where(lane == 0, jnp.concatenate([zero, r[:-1]], axis=0), r)
    after = jnp.where(lane == LANE - 1, jnp.concatenate([l[1:], zero], axis=0), l)
    return before, after


def stream(ref, a):
    lane = lax.broadcasted_iota(jnp.int32, (SUB, LANE), 1)
    blocks = ref.shape[0]
    r_old = l_old = r_far = None
    for j in range(blocks + 1):
        if j < blocks:
            v = ref[j, a : a + SUB]
            r = pltpu.roll(v, 1, axis=1)
            l = pltpu.roll(v, LANE - 1, axis=1)
        else:
            l = jnp.zeros((SUB, LANE), jnp.float32)
        if j > 0:
            before = jnp.where(lane == 0, r_far, r_old)
            after = jnp.where(lane == LANE - 1, l, l_old)
            yield j - 1, before, after
        r_far = r_old if j > 0 else jnp.zeros((SUB, LANE), jnp.float32)
        r_old, l_old = r, l


def all_around(ref, a):
    for j, before, after in stream(ref, a):
        yield j, (ref[j, a + 1 : a + 1 + SUB] + ref[j, a - 1 : a - 1 + SUB]) + (before + after)


def rows8(ref, a):
    return ref[:, a : a + SUB]


def neighbours(ref, a):
    before, after = rolled(rows8(ref, a))
    return (rows8(ref, a + 1) + rows8(ref, a - 1)) + (before + after)


def step_sizes(g):
    g00, g01, g02, g03, g11, g12, g13, g22, g23, g33 = g
    gram = [[g00, g01, g02, g03], [g01, g11, g12, g13], [g02, g12, g22, g23], [g03, g13, g23, g33]]

    def quad(c, left, right):
        total = None
        for i, ci in enumerate(c):
            for j, cj in enumerate(c):
                if left == right and j < i:
                    continue
                term = ci * cj * gram[i + left][j + right]
                if left == right and j > i:
                    term = 2.0 * term
                total = term if total is None else total + term
        return total

    coef = [jnp.ones_like(g00)]
    beta = [0.0, 0.0, 0.0]
    for sweep in range(3):
        rr = quad(coef, 0, 0)
        re = quad(coef, 0, 1)
        ee = quad(coef, 1, 1)
        inv = 1.0 / (jnp.maximum(rr + 2.0 * re + ee, 0.0) + EPSILON)
        s = (rr + re) * inv
        t = (re + ee + EPSILON) * inv
        for j, c in enumerate(coef):
            beta[j] = beta[j] + s * c
        nxt = [t * c for c in coef] + [jnp.zeros_like(s)]
        for j, c in enumerate(coef):
            nxt[j + 1] = nxt[j + 1] - s * c
        coef = nxt
    return beta


def meetings(tiles):
    bits = [1 << k for k in range((tiles - 1).bit_length())]
    known = {0, *bits}
    rounds = []
    while True:
        few = known | {1 ^ v for v in known}
        those = [1] if rounds and len(few) == tiles else bits
        known = known | {b ^ v for b in those for v in known}
        rounds.append(those)
        if len(known) == tiles:
            return rounds


def kernel(
    tiles, slices, rows, state_ref, depth_ref, press_ref, out_ref,
    raw, raw_d, raw_p, x, later, dm, dw, dw_before, dw_after, first_top, wfac, coarse, total, res, beside, sides_ref, c, u, top, out_c, out_y,
    part, slots, chain, chain_in,
    load_s, halo_s, halo_r, sum_s, sum_r, chain_s, chain_r, ready,
):
    me = lax.axis_index("tile")
    cut = lax.axis_index("cuts")
    has_lo = me > 0
    has_hi = me < tiles - 1
    has_prev = cut > 0
    has_next = cut < slices - 1
    blocks = x.shape[1]
    end = PAD + rows
    own = list(range(PAD, end, SUB))
    wide = list(range(PAD - 3, end - 5, SUB)) + [end - 5]
    wide = sorted(set(wide))

    loads = [
        pltpu.make_async_copy(state_ref.at[0], raw, load_s.at[0]),
        pltpu.make_async_copy(depth_ref, raw_d, load_s.at[1]),
        pltpu.make_async_copy(press_ref, raw_p, load_s.at[2]),
    ]
    for load in loads:
        load.start()

    barrier = pltpu.get_barrier_semaphore()
    cross = me + 2 * lax.rem(me, 2) - 1
    has_cross = (cross >= 0) & (cross < tiles)

    bits = [1 << k for k in range((tiles - 1).bit_length())]

    def partner(d):
        return me + sum(bit * (1 - 2 * lax.rem(me // bit, 2)) for bit in bits if d & bit)

    def tell(sem, bits):
        for bit in bits:
            pl.semaphore_signal(sem, inc=1, device_id={"tile": partner(bit)}, device_id_type=MESH)

    tell(barrier, bits)

    @pl.when(has_cross)
    def _():
        pl.semaphore_signal(barrier, inc=1, device_id={"tile": cross}, device_id_type=MESH)

    @pl.when(has_prev)
    def _():
        pl.semaphore_signal(barrier, inc=1, device_id={"cuts": cut - 1}, device_id_type=MESH)

    @pl.when(has_next)
    def _():
        pl.semaphore_signal(barrier, inc=1, device_id={"cuts": cut + 1}, device_id_type=MESH)

    for there, a in ((has_lo, 0), (has_hi, end)):

        @pl.when(jnp.logical_not(there))
        def _():
            x[:, :, a : a + PAD] = jnp.zeros((4, blocks, PAD, LANE), jnp.float32)

    for load in loads:
        load.wait()
    for j in range(blocks):
        cols = slice(j * LANE, (j + 1) * LANE)
        x[0, j, PAD:end] = raw[1, :, cols]
        x[1, j, PAD:end] = raw_d[:, cols]
        x[2, j, PAD:end] = raw[0, :, cols]
        x[3, j, PAD:end] = raw_p[:, cols]

    def halo_copy(k, side):
        p, count, a, size = PARTS[k]
        if side == 0:
            src, dst = PAD + a, end + a
        else:
            src, dst = end - a - size, PAD - a - size
        return pltpu.make_async_remote_copy(
            src_ref=x.at[pl.ds(p, count), :, pl.ds(src, size)],
            dst_ref=x.at[pl.ds(p, count), :, pl.ds(dst, size)],
            send_sem=halo_s.at[k, side],
            recv_sem=halo_r.at[k, side],
            device_id={"tile": me - 1 if side == 0 else me + 1},
            device_id_type=MESH,
        )

    def halo_both(ks, act):
        @pl.when(has_lo)
        def _():
            for k in ks:
                act(k, 0)

        @pl.when(has_hi)
        def _():
            for k in ks:
                act(k, 1)

    start = lambda k, side: halo_copy(k, side).start()
    arrive = lambda k, side: halo_copy(k, 1 - side).wait_recv()
    leave = lambda k, side: halo_copy(k, side).wait_send()

    def columns(a, inside=None):
        safe = rows8(x.at[1], a)
        if inside is not None:
            safe = jnp.where(inside, safe, 1.0)
        inv_depth = 1.0 / safe
        vert = LEVELS * inv_depth
        vert = vert * vert
        tops = None
        for m in range(LEVELS):
            inverse = 1.0 / (vert * LAM[m] - 4.0)
            if inside is not None:
                inverse = jnp.where(inside, inverse, 0.0)
            dm[m, :, a : a + SUB] = inverse
            dw[m, :, a : a + SUB] = WEIGHT[m] * inverse
            t = (TOPROW[m] * WEIGHT[m]) * inverse
            tops = t if tops is None else tops + t
        first_top[:, a : a + SUB] = tops
        wfac[:, a : a + SUB] = (0.5 * LEVELS) * inv_depth

    sub = lax.broadcasted_iota(jnp.int32, (1, SUB, LANE), 1)

    def edge_columns(a_lo, own_lo, a_hi, own_hi):
        columns(a_lo, sub + SUB * has_lo.astype(jnp.int32) >= own_lo)
        columns(a_hi, sub - SUB * has_hi.astype(jnp.int32) < own_hi)

    pl.semaphore_wait(
        barrier,
        len(bits)
        + has_cross.astype(jnp.int32)
        + has_prev.astype(jnp.int32)
        + has_next.astype(jnp.int32),
    )
    rounds = meetings(tiles)
    tell(ready.at[0], rounds[0])
    halo_both([0], start)

    for a in own:
        columns(a)
    depth = x[1, :, PAD:end]
    stiff = jnp.tanh(depth)
    z = TIME_STEP * TIME_STEP * stiff
    coarse[0] = 1.0 + z * (-1 / 2 + z * (1 / 24 + z * (-1 / 720 + z * (1 / 40320 - z / 3628800))))
    sine = TIME_STEP * (
        1.0 + z * (-1 / 6 + z * (1 / 120 + z * (-1 / 5040 + z * (1 / 362880 - z / 39916800))))
    )
    coarse[1] = stiff * sine
    coarse[2] = -sine

    for k in range(1, len(rounds)):
        pl.semaphore_wait(ready.at[k - 1], len(rounds[k - 1]))
        tell(ready.at[k], rounds[k])
    halo_both(NEAR_PARTS, start)

    halo_both([0], arrive)
    edge_columns(PAD - 4, 4, end - 4, 4)

    def sum_copy(s, d):
        return pltpu.make_async_remote_copy(
            src_ref=part.at[s],
            dst_ref=slots.at[s % 2, d - 1],
            send_sem=sum_s.at[s % 2, d - 1],
            recv_sem=sum_r.at[s % 2, d - 1],
            device_id={"tile": partner(d)},
            device_id_type=MESH,
        )

    half = lax.broadcasted_iota(jnp.int32, (1, LANE), 1) < LANE // 2

    def phi_of(s):
        return x.at[0] if s == 0 else later.at[s - 1, 0]

    def elev_of(s):
        return x.at[2] if s == 0 else later.at[s - 1, 1]

    def inner_products(s):
        phi = phi_of(s)
        for a in wide:
            res[:, a : a + SUB] = 4.0 * rows8(phi, a) - neighbours(phi, a)
        if s == 0:
            for a in wide:
                r = rows8(res, a)
                for m in range(LEVELS):
                    c[m, 0, :, a : a + SUB] = rows8(dw.at[m], a) * r
        else:
            for a in wide:
                for j, before, after in stream(res, a):
                    beside[0, j, a : a + SUB] = before
                    beside[1, j, a : a + SUB] = after
        gram = [None] * 10

        def add(k, v):
            gram[k] = v if gram[k] is None else gram[k] + v

        def first_power(ms, a, j):
            at, up, down = slice(a, a + SUB), slice(a + 1, a + 1 + SUB), slice(a - 1, a - 1 + SUB)
            r_up, r_down = res[j, up], res[j, down]
            before, after = beside[0, j, at], beside[1, j, at]
            for m in ms:
                v = (dw[m, j, up] * r_up + dw[m, j, down] * r_down) + (
                    dw_before[m, j, at] * before + dw_after[m, j, at] * after
                )
                u[m, 0, j, at] = v
                c[m, 1, j, at] = dm[m, j, at] * v

        def power(i, m, a):
            at = slice(a, a + SUB)
            for j, v in all_around(c.at[m, i], a):
                u[m, i, j, at] = v
                if i < 2:
                    c[m, i + 1, j, at] = dm[m, j, at] * v

        def products(ms, a, j):
            at = slice(a, a + SUB)
            if ms[0] == 0:
                sides = [None] * 6
            else:
                sides = [sides_ref[i, j, at] for i in range(6)]
            for m in ms:
                us = [u[m, i, j, at] for i in range(3)]
                k = 4
                for p in range(3):
                    for q in range(p, 3):
                        add(k, us[p] * us[q])
                        k += 1
                    w = WEIGHT[m] * us[p]
                    sides[p] = us[p] if m == 0 else sides[p] + us[p]
                    sides[3 + p] = w if m == 0 else sides[3 + p] + w
            if ms[-1] < LEVELS - 1:
                for i in range(6):
                    sides_ref[i, j, at] = sides[i]
                return
            u0 = res[j, at]
            add(0, u0 * u0)
            k = 4
            for p in range(3):
                add(1 + p, u0 * (sides[3 + p] + 0.125 * sides[p]))
                part_p = 0.125 * sides[p]
                for q in range(p, 3):
                    add(k, part_p * sides[q])
                    k += 1

        groups = [list(range(m, m + GROUP)) for m in range(0, LEVELS, GROUP)]

        def work(kind, ms):
            if kind == 0 and s > 0:
                return [functools.partial(first_power, ms, a, j) for a in wide for j in range(blocks)]
            if kind < 3:
                windows = own if kind == 2 else wide
                return [functools.partial(power, kind, m, a) for m in ms for a in windows]
            return [functools.partial(products, ms, a, j) for a in own for j in range(blocks)]

        for step in range(len(groups) + 3):
            tasks = []
            for kind in range(4):
                if 0 <= step - kind < len(groups):
                    todo = work(kind, groups[step - kind])
                    tasks += [((n + 0.5) / len(todo), kind, n, task) for n, task in enumerate(todo)]
            for _, _, _, task in sorted(tasks, key=lambda entry: entry[:3]):
                task()
        gram = [LEVELS * gram[0]] + [4.0 * g for g in gram[1:]]
        gram = [jnp.sum(g, axis=0, keepdims=True) for g in gram]
        for k in range(FOLD):
            a, b = gram[k], gram[k + FOLD]
            part[s, k : k + 1] = jnp.where(half, a, b) + pltpu.roll(
                jnp.where(half, b, a), LANE // 2, axis=1
            )

    def own_tops():
        for a in own:
            top[0, :, a : a + SUB] = rows8(first_top, a) * rows8(res, a)
            for i in range(1, 3):
                y = None
                for m in range(LEVELS):
                    v = TOPROW[m] * rows8(c.at[m, i], a)
                    y = v if y is None else y + v
                top[i, :, a : a + SUB] = y

    def beyond(s, regions):
        phi = phi_of(s)
        for side, (_, first_rows, second_row, _) in enumerate(regions):
            base = second_row - SUB
            for a in first_rows:
                r = 4.0 * rows8(phi, a) - neighbours(phi, a)
                for m in range(LEVELS):
                    out_c[m, side, 0, :, a - base : a - base + SUB] = rows8(dw.at[m], a) * r
        for m in range(LEVELS):
            for side, (_, _, second_row, _) in enumerate(regions):
                out_c[m, side, 1, :, SUB : 2 * SUB] = rows8(dm.at[m], second_row) * neighbours(
                    out_c.at[m, side, 0], SUB
                )
        for side, (_, _, second_row, third_row) in enumerate(regions):
            at = third_row - second_row + SUB
            ys = [None] * 3
            for m in range(LEVELS):
                c0, c1 = out_c.at[m, side, 0], out_c.at[m, side, 1]
                c2 = rows8(dm.at[m], third_row) * neighbours(c1, at)
                for i, v in enumerate([rows8(c0, at), rows8(c1, at), c2]):
                    v = TOPROW[m] * v
                    ys[i] = v if ys[i] is None else ys[i] + v
            for i in range(3):
                out_y[side, i] = ys[i]

    def explicit(s, a):
        elev, phi = elev_of(s), phi_of(s)
        before_h, after_h = rolled(rows8(elev, a))
        before_f, after_f = rolled(rows8(phi, a))
        he = 0.5 * (rows8(elev, a + 1) - rows8(elev, a - 1))
        fe = 0.5 * (rows8(phi, a + 1) - rows8(phi, a - 1))
        hn = 0.5 * (after_h - before_h)
        fn = 0.5 * (after_f - before_f)
        slope = 1.0 + he * he + hn * hn
        rate_h = SHIP_SPEED * he - (he * fe + hn * fn)
        rate_f = SHIP_SPEED * fe - rows8(elev, a) - 0.5 * (fe * fe + fn * fn) - rows8(x.at[3], a)
        return slope, rate_h, rate_f

    def rates(beta, y, known, a):
        slope, rate_h, rate_f = known
        w = (beta[0] * y[0] + beta[1] * y[1] + beta[2] * y[2]) * rows8(wfac, a)
        ws = w * slope
        return rate_h + ws, rate_f + 0.5 * w * ws

    def advance(s, a, rate_h, rate_f, there=None):
        ahead = TIME_STEP if s == STAGES - 2 else 0.5 * TIME_STEP
        new_f = rows8(x.at[0], a) + ahead * rate_f
        new_h = rows8(x.at[2], a) + ahead * rate_h
        if there is not None:
            new_f = jnp.where(there, new_f, 0.0)
            new_h = jnp.where(there, new_h, 0.0)
        later[s, 0, :, a : a + SUB] = new_f
        later[s, 1, :, a : a + SUB] = new_h

    near = [
        (has_lo, [PAD - 6], PAD - 6, PAD - 4),
        (has_hi, [end - 2], end - 2, end - 4),
    ]
    far = {
        0: [
            (has_lo, [PAD - 12, PAD - 10], PAD - 11, PAD - 12),
            (has_hi, [end + 2, end + 4], end + 3, end + 4),
        ],
        1: [
            (has_lo, [PAD - 10], PAD - 10, PAD - 12),
            (has_hi, [end + 2], end + 2, end + 4),
        ],
    }
    betas = []

    for s in range(STAGES):
        inner_products(s)
        if s == 0:
            pl.semaphore_wait(ready.at[len(rounds) - 1], len(rounds[-1]))
        for d in range(tiles - 1, 0, -1):
            sum_copy(s, d).start()
        if s > 0:
            for d in range(1, tiles):
                sum_copy(s - 1, d).wait_send()
        if s == STAGES - 1:
            halo_both(range(len(PARTS)), leave)
        own_tops()
        known = [explicit(s, a) for a in own] if s > 0 else None
        if s == 0:
            halo_both(FAR_PARTS, start)
            halo_both(NEAR_PARTS, arrive)
            edge_columns(PAD - 7, 7, end - 1, 1)
            known = [explicit(s, a) for a in own]
            for m in range(LEVELS):
                for a in wide:
                    before, after = rolled(rows8(dw.at[m], a))
                    dw_before[m, :, a : a + SUB] = before
                    dw_after[m, :, a : a + SUB] = after
        if s == 1:
            halo_both(FAR_PARTS, arrive)
            edge_columns(PAD - 13, SUB, end + 5, 0)
        if s - 1 in far:
            beyond(s - 1, far[s - 1])
            for side, (there, _, _, third_row) in enumerate(far[s - 1]):
                y = [out_y[side, i] for i in range(3)]
                seen = explicit(s - 1, third_row)
                rate_h, rate_f = rates(betas[s - 1], y, seen, third_row)
                advance(s - 1, third_row, rate_h, rate_f, there)
        if s < STAGES - 1:
            beyond(s, near)
            known_near = [explicit(s, third_row) for _, _, _, third_row in near]

        for d in range(1, tiles):
            sum_copy(s, d).wait_recv()
        whole = part[s]
        for d in range(1, tiles):
            whole = whole + slots[s % 2, d - 1]
        low = jnp.sum(jnp.where(half, whole, 0.0), axis=1, keepdims=True)
        high = jnp.sum(jnp.where(half, 0.0, whole), axis=1, keepdims=True)
        sums = [low[k : k + 1] for k in range(FOLD)] + [high[k : k + 1] for k in range(FOLD)]
        betas.append([jnp.broadcast_to(b, (SUB, LANE)) for b in step_sizes(sums)])

        if s < STAGES - 1:
            for side, (there, _, _, third_row) in enumerate(near):
                y = [out_y[side, i] for i in range(3)]
                rate_h, rate_f = rates(betas[s], y, known_near[side], third_row)
                advance(s, third_row, rate_h, rate_f, there)
        share = (1.0 if s in (0, STAGES - 1) else 2.0) * (TIME_STEP / 6.0)
        for a, seen in zip(own, known):
            y = [rows8(top.at[i], a) for i in range(3)]
            rate_h, rate_f = rates(betas[s], y, seen, a)
            if s < STAGES - 1:
                advance(s, a, rate_h, rate_f)
            b = a - PAD
            if s == 0:
                total[0, :, b : b + SUB] = rows8(x.at[2], a) + share * rate_h
                total[1, :, b : b + SUB] = rows8(x.at[0], a) + share * rate_f
            else:
                total[0, :, b : b + SUB] += share * rate_h
                total[1, :, b : b + SUB] += share * rate_f

    chunk = 2
    pieces = list(range(0, blocks, chunk))

    def chain_copy(k):
        return pltpu.make_async_remote_copy(
            src_ref=chain.at[pl.ds(pieces[k], chunk)],
            dst_ref=chain_in.at[pl.ds(pieces[k], chunk)],
            send_sem=chain_s.at[k],
            recv_sem=chain_r.at[k],
            device_id={"cuts": cut + 1},
            device_id_type=MESH,
        )

    @pl.when(has_prev)
    def _():
        e = x[2, :, PAD:end]
        p = x[0, :, PAD:end]
        total[0] = total[0] - (coarse[0] * e + coarse[1] * p)
        total[1] = total[1] - (coarse[2] * e + coarse[0] * p)

    for k, first in enumerate(pieces):
        span = slice(first, first + chunk)

        @pl.when(has_prev)
        def _():
            chain_copy(k).wait_recv()
            e = chain_in[span, 0]
            p = chain_in[span, 1]
            chain[span, 0] = coarse[0, span] * e + coarse[1, span] * p + total[0, span]
            chain[span, 1] = coarse[2, span] * e + coarse[0, span] * p + total[1, span]

        @pl.when(jnp.logical_not(has_prev))
        def _():
            chain[span, 0] = total[0, span]
            chain[span, 1] = total[1, span]

        @pl.when(has_next)
        def _():
            chain_copy(k).start()

    for j in range(blocks):
        for k in range(2):
            out_ref[0, k, :, j * LANE : (j + 1) * LANE] = chain[j, k]

    @pl.when(has_next)
    def _():
        for k in range(len(pieces)):
            chain_copy(k).wait_send()

    for d in range(1, tiles):
        sum_copy(STAGES - 1, d).wait_send()


def local(tiles, slices, state_in, sea_depth, pressure):
    rows, columns = sea_depth.shape
    blocks = columns // LANE
    field = (blocks, rows + 2 * PAD, LANE)
    plane = (blocks, rows, LANE)
    f32 = jnp.float32
    pieces = blocks // 2
    return pl.pallas_call(
        functools.partial(kernel, tiles, slices, rows),
        out_shape=jax.ShapeDtypeStruct(state_in.shape, f32),
        in_specs=[pl.BlockSpec(memory_space=pltpu.HBM)] * 3,
        out_specs=pl.BlockSpec(memory_space=pltpu.VMEM),
        scratch_shapes=[
            pltpu.VMEM(state_in.shape[1:], f32),
            pltpu.VMEM(sea_depth.shape, f32),
            pltpu.VMEM(pressure.shape, f32),
            pltpu.VMEM((4,) + field, f32),
            pltpu.VMEM((STAGES - 1, 2) + field, f32),
            pltpu.VMEM((LEVELS,) + field, f32),
            pltpu.VMEM((LEVELS,) + field, f32),
            pltpu.VMEM((LEVELS,) + field, f32),
            pltpu.VMEM((LEVELS,) + field, f32),
            pltpu.VMEM(field, f32),
            pltpu.VMEM(field, f32),
            pltpu.VMEM((3,) + plane, f32),
            pltpu.VMEM((2,) + plane, f32),
            pltpu.VMEM(field, f32),
            pltpu.VMEM((2,) + field, f32),
            pltpu.VMEM((6,) + field, f32),
            pltpu.VMEM((LEVELS, 3) + field, f32),
            pltpu.VMEM((LEVELS, 3) + field, f32),
            pltpu.VMEM((3,) + field, f32),
            pltpu.VMEM((LEVELS, 2, 2, blocks, SPAN, LANE), f32),
            pltpu.VMEM((2, 3, blocks, SUB, LANE), f32),
            pltpu.VMEM((STAGES, FOLD, LANE), f32),
            pltpu.VMEM((2, tiles - 1, FOLD, LANE), f32),
            pltpu.VMEM((blocks, 2, rows, LANE), f32),
            pltpu.VMEM((blocks, 2, rows, LANE), f32),
            pltpu.SemaphoreType.DMA((3,)),
            pltpu.SemaphoreType.DMA((len(PARTS), 2)),
            pltpu.SemaphoreType.DMA((len(PARTS), 2)),
            pltpu.SemaphoreType.DMA((2, tiles - 1)),
            pltpu.SemaphoreType.DMA((2, tiles - 1)),
            pltpu.SemaphoreType.DMA((pieces,)),
            pltpu.SemaphoreType.DMA((pieces,)),
            pltpu.SemaphoreType.REGULAR((len(meetings(tiles)),)),
        ],
        compiler_params=pltpu.CompilerParams(
            collective_id=0, has_side_effects=True, vmem_limit_bytes=60 * 1024 * 1024
        ),
        name="wake_step",
    )(state_in, sea_depth, pressure)


def solution(mesh):
    placed = (P("cuts", None, "tile", None), P("tile", None), P("tile", None))
    return jax.shard_map(
        functools.partial(local, mesh.shape["tile"], mesh.shape["cuts"]),
        mesh=mesh,
        in_specs=placed,
        out_specs=P("cuts", None, "tile", None),
        check_vma=False,
    )
```

```python
import functools
import math

import jax
import jax.numpy as jnp
from jax import lax
from jax.experimental import pallas as pl
from jax.experimental.pallas import tpu as pltpu
from jax.sharding import PartitionSpec as P

LEVELS = 8
STAGES = 4
TIME_STEP = 0.8
SHIP_SPEED = 0.5
EPSILON = 1e-06
MESH = pl.DeviceIdType.MESH
SUB = 8
LANE = 128
FOLD = 5
PAD = 16
SPAN = 24
GROUP = 4
PARTS = [(0, 2, 0, 4), (0, 2, 4, 3), (2, 2, 0, 5), (0, 2, 7, 6), (2, 2, 5, 6)]
NEAR_PARTS = [1, 2]
FAR_PARTS = [3, 4]

THETA = [(m + 0.5) * math.pi / LEVELS for m in range(LEVELS)]
LAM = [2.0 * math.cos(t) - 2.0 for t in THETA]
WEIGHT = [(-1.0) ** m / math.tan(t / 2) / LEVELS for m, t in enumerate(THETA)]
TOPROW = [math.cos((LEVELS - 2) * t) - 4.0 * math.cos((LEVELS - 1) * t) for t in THETA]


def rolled(v):
    lane = lax.broadcasted_iota(jnp.int32, (1,) + v.shape[1:], 2)
    r = pltpu.roll(v, 1, axis=2)
    l = pltpu.roll(v, LANE - 1, axis=2)
    zero = jnp.zeros_like(v[:1])
    before = jnp.where(lane == 0, jnp.concatenate([zero, r[:-1]], axis=0), r)
    after = jnp.where(lane == LANE - 1, jnp.concatenate([l[1:], zero], axis=0), l)
    return before, after


def stream(ref, a):
    lane = lax.broadcasted_iota(jnp.int32, (SUB, LANE), 1)
    blocks = ref.shape[0]
    r_old = l_old = r_far = None
    for j in range(blocks + 1):
        if j < blocks:
            v = ref[j, a : a + SUB]
            r = pltpu.roll(v, 1, axis=1)
            l = pltpu.roll(v, LANE - 1, axis=1)
        else:
            l = jnp.zeros((SUB, LANE), jnp.float32)
        if j > 0:
            before = jnp.where(lane == 0, r_far, r_old)
            after = jnp.where(lane == LANE - 1, l, l_old)
            yield j - 1, before, after
        r_far = r_old if j > 0 else jnp.zeros((SUB, LANE), jnp.float32)
        r_old, l_old = r, l


def all_around(ref, a):
    for j, before, after in stream(ref, a):
        yield j, (ref[j, a + 1 : a + 1 + SUB] + ref[j, a - 1 : a - 1 + SUB]) + (before + after)


def rows8(ref, a):
    return ref[:, a : a + SUB]


def neighbours(ref, a):
    before, after = rolled(rows8(ref, a))
    return (rows8(ref, a + 1) + rows8(ref, a - 1)) + (before + after)


def step_sizes(g):
    g00, g01, g02, g03, g11, g12, g13, g22, g23, g33 = g
    gram = [[g00, g01, g02, g03], [g01, g11, g12, g13], [g02, g12, g22, g23], [g03, g13, g23, g33]]

    def quad(c, left, right):
        total = None
        for i, ci in enumerate(c):
            for j, cj in enumerate(c):
                if left == right and j < i:
                    continue
                term = ci * cj * gram[i + left][j + right]
                if left == right and j > i:
                    term = 2.0 * term
                total = term if total is None else total + term
        return total

    coef = [jnp.ones_like(g00)]
    beta = [0.0, 0.0, 0.0]
    for sweep in range(3):
        rr = quad(coef, 0, 0)
        re = quad(coef, 0, 1)
        ee = quad(coef, 1, 1)
        inv = 1.0 / (jnp.maximum(rr + 2.0 * re + ee, 0.0) + EPSILON)
        s = (rr + re) * inv
        t = (re + ee + EPSILON) * inv
        for j, c in enumerate(coef):
            beta[j] = beta[j] + s * c
        nxt = [t * c for c in coef] + [jnp.zeros_like(s)]
        for j, c in enumerate(coef):
            nxt[j + 1] = nxt[j + 1] - s * c
        coef = nxt
    return beta


def meetings(tiles):
    bits = [1 << k for k in range((tiles - 1).bit_length())]
    known = {0, *bits}
    rounds = []
    while True:
        few = known | {1 ^ v for v in known}
        those = [1] if rounds and len(few) == tiles else bits
        known = known | {b ^ v for b in those for v in known}
        rounds.append(those)
        if len(known) == tiles:
            return rounds


def kernel(
    tiles, slices, rows, state_ref, depth_ref, press_ref, out_ref,
    raw, raw_d, raw_p, x, later, dm, dw, dw_before, dw_after, first_top, wfac, coarse, total, res, beside, sides_ref, c, u, top, out_c, out_y,
    part, slots, chain, chain_in,
    load_s, halo_s, halo_r, sum_s, sum_r, chain_s, chain_r, ready,
):
    me = lax.axis_index("tile")
    cut = lax.axis_index("cuts")
    has_lo = me > 0
    has_hi = me < tiles - 1
    has_prev = cut > 0
    has_next = cut < slices - 1
    blocks = x.shape[1]
    end = PAD + rows
    own = list(range(PAD, end, SUB))
    wide = list(range(PAD - 3, end - 5, SUB)) + [end - 5]
    wide = sorted(set(wide))

    loads = [
        pltpu.make_async_copy(state_ref.at[0], raw, load_s.at[0]),
        pltpu.make_async_copy(depth_ref, raw_d, load_s.at[1]),
        pltpu.make_async_copy(press_ref, raw_p, load_s.at[2]),
    ]
    for load in loads:
        load.start()

    barrier = pltpu.get_barrier_semaphore()
    cross = me + 2 * lax.rem(me, 2) - 1
    has_cross = (cross >= 0) & (cross < tiles)

    bits = [1 << k for k in range((tiles - 1).bit_length())]

    def partner(d):
        return me + sum(bit * (1 - 2 * lax.rem(me // bit, 2)) for bit in bits if d & bit)

    def tell(sem, bits):
        for bit in bits:
            pl.semaphore_signal(sem, inc=1, device_id={"tile": partner(bit)}, device_id_type=MESH)

    tell(barrier, bits)

    @pl.when(has_cross)
    def _():
        pl.semaphore_signal(barrier, inc=1, device_id={"tile": cross}, device_id_type=MESH)

    @pl.when(has_prev)
    def _():
        pl.semaphore_signal(barrier, inc=1, device_id={"cuts": cut - 1}, device_id_type=MESH)

    @pl.when(has_next)
    def _():
        pl.semaphore_signal(barrier, inc=1, device_id={"cuts": cut + 1}, device_id_type=MESH)

    for there, a in ((has_lo, 0), (has_hi, end)):

        @pl.when(jnp.logical_not(there))
        def _():
            x[:, :, a : a + PAD] = jnp.zeros((4, blocks, PAD, LANE), jnp.float32)

    for load in loads:
        load.wait()
    for j in range(blocks):
        cols = slice(j * LANE, (j + 1) * LANE)
        x[0, j, PAD:end] = raw[1, :, cols]
        x[1, j, PAD:end] = raw_d[:, cols]
        x[2, j, PAD:end] = raw[0, :, cols]
        x[3, j, PAD:end] = raw_p[:, cols]

    def halo_copy(k, side):
        p, count, a, size = PARTS[k]
        if side == 0:
            src, dst = PAD + a, end + a
        else:
            src, dst = end - a - size, PAD - a - size
        return pltpu.make_async_remote_copy(
            src_ref=x.at[pl.ds(p, count), :, pl.ds(src, size)],
            dst_ref=x.at[pl.ds(p, count), :, pl.ds(dst, size)],
            send_sem=halo_s.at[k, side],
            recv_sem=halo_r.at[k, side],
            device_id={"tile": me - 1 if side == 0 else me + 1},
            device_id_type=MESH,
        )

    def halo_both(ks, act):
        @pl.when(has_lo)
        def _():
            for k in ks:
                act(k, 0)

        @pl.when(has_hi)
        def _():
            for k in ks:
                act(k, 1)

    start = lambda k, side: halo_copy(k, side).start()
    arrive = lambda k, side: halo_copy(k, 1 - side).wait_recv()
    leave = lambda k, side: halo_copy(k, side).wait_send()

    def columns(a, inside=None):
        safe = rows8(x.at[1], a)
        if inside is not None:
            safe = jnp.where(inside, safe, 1.0)
        inv_depth = 1.0 / safe
        vert = LEVELS * inv_depth
        vert = vert * vert
        tops = None
        for m in range(LEVELS):
            inverse = 1.0 / (vert * LAM[m] - 4.0)
            if inside is not None:
                inverse = jnp.where(inside, inverse, 0.0)
            dm[m, :, a : a + SUB] = inverse
            dw[m, :, a : a + SUB] = WEIGHT[m] * inverse
            t = (TOPROW[m] * WEIGHT[m]) * inverse
            tops = t if tops is None else tops + t
        first_top[:, a : a + SUB] = tops
        wfac[:, a : a + SUB] = (0.5 * LEVELS) * inv_depth

    sub = lax.broadcasted_iota(jnp.int32, (1, SUB, LANE), 1)

    def edge_columns(a_lo, own_lo, a_hi, own_hi):
        columns(a_lo, sub + SUB * has_lo.astype(jnp.int32) >= own_lo)
        columns(a_hi, sub - SUB * has_hi.astype(jnp.int32) < own_hi)

    pl.semaphore_wait(
        barrier,
        len(bits)
        + has_cross.astype(jnp.int32)
        + has_prev.astype(jnp.int32)
        + has_next.astype(jnp.int32),
    )
    rounds = meetings(tiles)
    tell(ready.at[0], rounds[0])
    halo_both([0], start)

    for a in own:
        columns(a)
    depth = x[1, :, PAD:end]
    stiff = jnp.tanh(depth)
    z = TIME_STEP * TIME_STEP * stiff
    coarse[0] = 1.0 + z * (-1 / 2 + z * (1 / 24 + z * (-1 / 720 + z * (1 / 40320 - z / 3628800))))
    sine = TIME_STEP * (
        1.0 + z * (-1 / 6 + z * (1 / 120 + z * (-1 / 5040 + z * (1 / 362880 - z / 39916800))))
    )
    coarse[1] = stiff * sine
    coarse[2] = -sine

    for k in range(1, len(rounds)):
        pl.semaphore_wait(ready.at[k - 1], len(rounds[k - 1]))
        tell(ready.at[k], rounds[k])
    halo_both(NEAR_PARTS, start)

    halo_both([0], arrive)
    edge_columns(PAD - 4, 4, end - 4, 4)

    def sum_copy(s, d):
        return pltpu.make_async_remote_copy(
            src_ref=part.at[s],
            dst_ref=slots.at[s % 2, d - 1],
            send_sem=sum_s.at[s % 2, d - 1],
            recv_sem=sum_r.at[s % 2, d - 1],
            device_id={"tile": partner(d)},
            device_id_type=MESH,
        )

    half = lax.broadcasted_iota(jnp.int32, (1, LANE), 1) < LANE // 2

    def phi_of(s):
        return x.at[0] if s == 0 else later.at[s - 1, 0]

    def elev_of(s):
        return x.at[2] if s == 0 else later.at[s - 1, 1]

    def inner_products(s):
        phi = phi_of(s)
        for a in wide:
            res[:, a : a + SUB] = 4.0 * rows8(phi, a) - neighbours(phi, a)
        if s == 0:
            for a in wide:
                r = rows8(res, a)
                for m in range(LEVELS):
                    c[m, 0, :, a : a + SUB] = rows8(dw.at[m], a) * r
        else:
            for a in wide:
                for j, before, after in stream(res, a):
                    beside[0, j, a : a + SUB] = before
                    beside[1, j, a : a + SUB] = after
        gram = [None] * 10

        def add(k, v):
            gram[k] = v if gram[k] is None else gram[k] + v

        def first_power(ms, a, j):
            at, up, down = slice(a, a + SUB), slice(a + 1, a + 1 + SUB), slice(a - 1, a - 1 + SUB)
            r_up, r_down = res[j, up], res[j, down]
            before, after = beside[0, j, at], beside[1, j, at]
            for m in ms:
                v = (dw[m, j, up] * r_up + dw[m, j, down] * r_down) + (
                    dw_before[m, j, at] * before + dw_after[m, j, at] * after
                )
                u[m, 0, j, at] = v
                c[m, 1, j, at] = dm[m, j, at] * v

        def power(i, m, a):
            at = slice(a, a + SUB)
            for j, v in all_around(c.at[m, i], a):
                u[m, i, j, at] = v
                if i < 2:
                    c[m, i + 1, j, at] = dm[m, j, at] * v

        def products(ms, a, j):
            at = slice(a, a + SUB)
            if ms[0] == 0:
                sides = [None] * 6
            else:
                sides = [sides_ref[i, j, at] for i in range(6)]
            for m in ms:
                us = [u[m, i, j, at] for i in range(3)]
                k = 4
                for p in range(3):
                    for q in range(p, 3):
                        add(k, us[p] * us[q])
                        k += 1
                    w = WEIGHT[m] * us[p]
                    sides[p] = us[p] if m == 0 else sides[p] + us[p]
                    sides[3 + p] = w if m == 0 else sides[3 + p] + w
            if ms[-1] < LEVELS - 1:
                for i in range(6):
                    sides_ref[i, j, at] = sides[i]
                return
            u0 = res[j, at]
            add(0, u0 * u0)
            k = 4
            for p in range(3):
                add(1 + p, u0 * (sides[3 + p] + 0.125 * sides[p]))
                part_p = 0.125 * sides[p]
                for q in range(p, 3):
                    add(k, part_p * sides[q])
                    k += 1

        groups = [list(range(m, m + GROUP)) for m in range(0, LEVELS, GROUP)]

        def work(kind, ms):
            if kind == 0 and s > 0:
                return [functools.partial(first_power, ms, a, j) for a in wide for j in range(blocks)]
            if kind < 3:
                windows = own if kind == 2 else wide
                return [functools.partial(power, kind, m, a) for m in ms for a in windows]
            return [functools.partial(products, ms, a, j) for a in own for j in range(blocks)]

        for step in range(len(groups) + 3):
            tasks = []
            for kind in range(4):
                if 0 <= step - kind < len(groups):
                    todo = work(kind, groups[step - kind])
                    tasks += [((n + 0.5) / len(todo), kind, n, task) for n, task in enumerate(todo)]
            for _, _, _, task in sorted(tasks, key=lambda entry: entry[:3]):
                task()
        gram = [LEVELS * gram[0]] + [4.0 * g for g in gram[1:]]
        gram = [jnp.sum(g, axis=0, keepdims=True) for g in gram]
        for k in range(FOLD):
            a, b = gram[k], gram[k + FOLD]
            part[s, k : k + 1] = jnp.where(half, a, b) + pltpu.roll(
                jnp.where(half, b, a), LANE // 2, axis=1
            )

    def own_tops():
        for a in own:
            top[0, :, a : a + SUB] = rows8(first_top, a) * rows8(res, a)
            for i in range(1, 3):
                y = None
                for m in range(LEVELS):
                    v = TOPROW[m] * rows8(c.at[m, i], a)
                    y = v if y is None else y + v
                top[i, :, a : a + SUB] = y

    def beyond(s, regions):
        phi = phi_of(s)
        for side, (_, first_rows, second_row, _) in enumerate(regions):
            base = second_row - SUB
            for a in first_rows:
                r = 4.0 * rows8(phi, a) - neighbours(phi, a)
                for m in range(LEVELS):
                    out_c[m, side, 0, :, a - base : a - base + SUB] = rows8(dw.at[m], a) * r
        for m in range(LEVELS):
            for side, (_, _, second_row, _) in enumerate(regions):
                out_c[m, side, 1, :, SUB : 2 * SUB] = rows8(dm.at[m], second_row) * neighbours(
                    out_c.at[m, side, 0], SUB
                )
        for side, (_, _, second_row, third_row) in enumerate(regions):
            at = third_row - second_row + SUB
            ys = [None] * 3
            for m in range(LEVELS):
                c0, c1 = out_c.at[m, side, 0], out_c.at[m, side, 1]
                c2 = rows8(dm.at[m], third_row) * neighbours(c1, at)
                for i, v in enumerate([rows8(c0, at), rows8(c1, at), c2]):
                    v = TOPROW[m] * v
                    ys[i] = v if ys[i] is None else ys[i] + v
            for i in range(3):
                out_y[side, i] = ys[i]

    def explicit(s, a):
        elev, phi = elev_of(s), phi_of(s)
        before_h, after_h = rolled(rows8(elev, a))
        before_f, after_f = rolled(rows8(phi, a))
        he = 0.5 * (rows8(elev, a + 1) - rows8(elev, a - 1))
        fe = 0.5 * (rows8(phi, a + 1) - rows8(phi, a - 1))
        hn = 0.5 * (after_h - before_h)
        fn = 0.5 * (after_f - before_f)
        slope = 1.0 + he * he + hn * hn
        rate_h = SHIP_SPEED * he - (he * fe + hn * fn)
        rate_f = SHIP_SPEED * fe - rows8(elev, a) - 0.5 * (fe * fe + fn * fn) - rows8(x.at[3], a)
        return slope, rate_h, rate_f

    def rates(beta, y, known, a):
        slope, rate_h, rate_f = known
        w = (beta[0] * y[0] + beta[1] * y[1] + beta[2] * y[2]) * rows8(wfac, a)
        ws = w * slope
        return rate_h + ws, rate_f + 0.5 * w * ws

    def advance(s, a, rate_h, rate_f, there=None):
        ahead = TIME_STEP if s == STAGES - 2 else 0.5 * TIME_STEP
        new_f = rows8(x.at[0], a) + ahead * rate_f
        new_h = rows8(x.at[2], a) + ahead * rate_h
        if there is not None:
            new_f = jnp.where(there, new_f, 0.0)
            new_h = jnp.where(there, new_h, 0.0)
        later[s, 0, :, a : a + SUB] = new_f
        later[s, 1, :, a : a + SUB] = new_h

    near = [
        (has_lo, [PAD - 6], PAD - 6, PAD - 4),
        (has_hi, [end - 2], end - 2, end - 4),
    ]
    far = {
        0: [
            (has_lo, [PAD - 12, PAD - 10], PAD - 11, PAD - 12),
            (has_hi, [end + 2, end + 4], end + 3, end + 4),
        ],
        1: [
            (has_lo, [PAD - 10], PAD - 10, PAD - 12),
            (has_hi, [end + 2], end + 2, end + 4),
        ],
    }
    betas = []

    for s in range(STAGES):
        inner_products(s)
        if s == 0:
            pl.semaphore_wait(ready.at[len(rounds) - 1], len(rounds[-1]))
        for d in range(tiles - 1, 0, -1):
            sum_copy(s, d).start()
        if s > 0:
            for d in range(1, tiles):
                sum_copy(s - 1, d).wait_send()
        if s == STAGES - 1:
            halo_both(range(len(PARTS)), leave)
        own_tops()
        known = [explicit(s, a) for a in own] if s > 0 else None
        if s == 0:
            halo_both(FAR_PARTS, start)
            halo_both(NEAR_PARTS, arrive)
            edge_columns(PAD - 7, 7, end - 1, 1)
            known = [explicit(s, a) for a in own]
            for m in range(LEVELS):
                for a in wide:
                    before, after = rolled(rows8(dw.at[m], a))
                    dw_before[m, :, a : a + SUB] = before
                    dw_after[m, :, a : a + SUB] = after
        if s == 1:
            halo_both(FAR_PARTS, arrive)
            edge_columns(PAD - 13, SUB, end + 5, 0)
        if s - 1 in far:
            beyond(s - 1, far[s - 1])
            for side, (there, _, _, third_row) in enumerate(far[s - 1]):
                y = [out_y[side, i] for i in range(3)]
                seen = explicit(s - 1, third_row)
                rate_h, rate_f = rates(betas[s - 1], y, seen, third_row)
                advance(s - 1, third_row, rate_h, rate_f, there)
        if s < STAGES - 1:
            beyond(s, near)
            known_near = [explicit(s, third_row) for _, _, _, third_row in near]

        for d in range(1, tiles):
            sum_copy(s, d).wait_recv()
        whole = part[s]
        for d in range(1, tiles):
            whole = whole + slots[s % 2, d - 1]
        low = jnp.sum(jnp.where(half, whole, 0.0), axis=1, keepdims=True)
        high = jnp.sum(jnp.where(half, 0.0, whole), axis=1, keepdims=True)
        sums = [low[k : k + 1] for k in range(FOLD)] + [high[k : k + 1] for k in range(FOLD)]
        betas.append([jnp.broadcast_to(b, (SUB, LANE)) for b in step_sizes(sums)])

        if s < STAGES - 1:
            for side, (there, _, _, third_row) in enumerate(near):
                y = [out_y[side, i] for i in range(3)]
                rate_h, rate_f = rates(betas[s], y, known_near[side], third_row)
                advance(s, third_row, rate_h, rate_f, there)
        share = (1.0 if s in (0, STAGES - 1) else 2.0) * (TIME_STEP / 6.0)
        for a, seen in zip(own, known):
            y = [rows8(top.at[i], a) for i in range(3)]
            rate_h, rate_f = rates(betas[s], y, seen, a)
            if s < STAGES - 1:
                advance(s, a, rate_h, rate_f)
            b = a - PAD
            if s == 0:
                total[0, :, b : b + SUB] = rows8(x.at[2], a) + share * rate_h
                total[1, :, b : b + SUB] = rows8(x.at[0], a) + share * rate_f
            else:
                total[0, :, b : b + SUB] += share * rate_h
                total[1, :, b : b + SUB] += share * rate_f

    chunk = 2
    pieces = list(range(0, blocks, chunk))

    def chain_copy(k):
        return pltpu.make_async_remote_copy(
            src_ref=chain.at[pl.ds(pieces[k], chunk)],
            dst_ref=chain_in.at[pl.ds(pieces[k], chunk)],
            send_sem=chain_s.at[k],
            recv_sem=chain_r.at[k],
            device_id={"cuts": cut + 1},
            device_id_type=MESH,
        )

    @pl.when(has_prev)
    def _():
        e = x[2, :, PAD:end]
        p = x[0, :, PAD:end]
        total[0] = total[0] - (coarse[0] * e + coarse[1] * p)
        total[1] = total[1] - (coarse[2] * e + coarse[0] * p)

    for k, first in enumerate(pieces):
        span = slice(first, first + chunk)

        @pl.when(has_prev)
        def _():
            chain_copy(k).wait_recv()
            e = chain_in[span, 0]
            p = chain_in[span, 1]
            chain[span, 0] = coarse[0, span] * e + coarse[1, span] * p + total[0, span]
            chain[span, 1] = coarse[2, span] * e + coarse[0, span] * p + total[1, span]

        @pl.when(jnp.logical_not(has_prev))
        def _():
            chain[span, 0] = total[0, span]
            chain[span, 1] = total[1, span]

        @pl.when(has_next)
        def _():
            chain_copy(k).start()

        for j in range(first, first + chunk):
            for i in range(2):
                out_ref[0, i, :, j * LANE : (j + 1) * LANE] = chain[j, i]

    @pl.when(has_next)
    def _():
        for k in range(len(pieces)):
            chain_copy(k).wait_send()

    for d in range(1, tiles):
        sum_copy(STAGES - 1, d).wait_send()


def local(tiles, slices, state_in, sea_depth, pressure):
    rows, columns = sea_depth.shape
    blocks = columns // LANE
    field = (blocks, rows + 2 * PAD, LANE)
    plane = (blocks, rows, LANE)
    f32 = jnp.float32
    pieces = blocks // 2
    return pl.pallas_call(
        functools.partial(kernel, tiles, slices, rows),
        out_shape=jax.ShapeDtypeStruct(state_in.shape, f32),
        in_specs=[pl.BlockSpec(memory_space=pltpu.HBM)] * 3,
        out_specs=pl.BlockSpec(memory_space=pltpu.VMEM),
        scratch_shapes=[
            pltpu.VMEM(state_in.shape[1:], f32),
            pltpu.VMEM(sea_depth.shape, f32),
            pltpu.VMEM(pressure.shape, f32),
            pltpu.VMEM((4,) + field, f32),
            pltpu.VMEM((STAGES - 1, 2) + field, f32),
            pltpu.VMEM((LEVELS,) + field, f32),
            pltpu.VMEM((LEVELS,) + field, f32),
            pltpu.VMEM((LEVELS,) + field, f32),
            pltpu.VMEM((LEVELS,) + field, f32),
            pltpu.VMEM(field, f32),
            pltpu.VMEM(field, f32),
            pltpu.VMEM((3,) + plane, f32),
            pltpu.VMEM((2,) + plane, f32),
            pltpu.VMEM(field, f32),
            pltpu.VMEM((2,) + field, f32),
            pltpu.VMEM((6,) + field, f32),
            pltpu.VMEM((LEVELS, 3) + field, f32),
            pltpu.VMEM((LEVELS, 3) + field, f32),
            pltpu.VMEM((3,) + field, f32),
            pltpu.VMEM((LEVELS, 2, 2, blocks, SPAN, LANE), f32),
            pltpu.VMEM((2, 3, blocks, SUB, LANE), f32),
            pltpu.VMEM((STAGES, FOLD, LANE), f32),
            pltpu.VMEM((2, tiles - 1, FOLD, LANE), f32),
            pltpu.VMEM((blocks, 2, rows, LANE), f32),
            pltpu.VMEM((blocks, 2, rows, LANE), f32),
            pltpu.SemaphoreType.DMA((3,)),
            pltpu.SemaphoreType.DMA((len(PARTS), 2)),
            pltpu.SemaphoreType.DMA((len(PARTS), 2)),
            pltpu.SemaphoreType.DMA((2, tiles - 1)),
            pltpu.SemaphoreType.DMA((2, tiles - 1)),
            pltpu.SemaphoreType.DMA((pieces,)),
            pltpu.SemaphoreType.DMA((pieces,)),
            pltpu.SemaphoreType.REGULAR((len(meetings(tiles)),)),
        ],
        compiler_params=pltpu.CompilerParams(
            collective_id=0, has_side_effects=True, vmem_limit_bytes=60 * 1024 * 1024
        ),
        name="wake_step",
    )(state_in, sea_depth, pressure)


def solution(mesh):
    placed = (P("cuts", None, "tile", None), P("tile", None), P("tile", None))
    return jax.shard_map(
        functools.partial(local, mesh.shape["tile"], mesh.shape["cuts"]),
        mesh=mesh,
        in_specs=placed,
        out_specs=P("cuts", None, "tile", None),
        check_vma=False,
    )
```
